32 devices in a mesh: chol: 8 (over z, y), walk: 4 (over x, core).
Axes of the slice: x: 2, y: 2, z: 4, core: 2. Of those that a mesh axis runs over, the one named last changes fastest.
Arguments:
- green: bfloat16 [32, 128, 512], P(('chol', 'walk')), may hold values from -2 to 2
- cholesky_rotated_vectors: bfloat16 [32, 128, 512], P('chol'), may hold values from -0.25 to 0.25
- walker_weight: float32 [32], P(('chol', 'walk')), may hold values from 0.04 to 0.16
Outputs:
- green_cot: float32 [32, 128, 512], P(('chol', 'walk'))
- chol_grad: float32 [32, 128, 512], P('chol', None, 'walk')
The draws below stay inside these ranges and needn't reach their ends.
All inputs are finite; a program needn't handle non-finite values.
Results may differ from the reference program's by a relative error of at most 0.0029.
Values may be sent and summed in bfloat16 or wider, within the bound.
A program may use at most 64 MiB of HBM per device.

```python
import math
import jax
import jax.numpy as jnp
from jax import lax

O = 128
M = 512
NV = 32
WALKERS = 32


def levels(rng, extent, split, low, top_value):
    factor_of = 1.0
    for dim, parts in split:
        heights = jax.random.uniform(jax.random.fold_in(jax.random.fold_in(rng, 6), dim), (parts,), jnp.float32, low / len(split), top_value / len(split))
        factor_of = factor_of * jnp.repeat(jnp.exp(heights), extent[dim] // parts).reshape((-1,) + (1,) * (len(extent) - 1 - dim))
    return factor_of


def normal_values(key, shape, deviation, bound, pieces=(), held_as=jnp.bfloat16):
    entries = deviation * jax.random.normal(key, shape, jnp.float32)
    if pieces:
        entries = entries * levels(key, shape, pieces, -0.22, 0.18)
    return jnp.clip(entries, -bound, bound).astype(held_as)


def setup_inputs(seed: int = 0) -> dict:
    streams_of = jax.random.split(jax.random.key(seed), 4)
    green = normal_values(streams_of[0], (WALKERS, O, M), 0.35, 2.0, ((0, 32),))
    cholesky_rotated_vectors = normal_values(streams_of[1], (NV, O, M), M ** -0.5, 0.25, ((0, 8),))
    walker_weight = jnp.clip(jnp.exp(math.log(0.16) - 1.3862944 * jax.random.uniform(streams_of[2], (WALKERS,), jnp.float32) ** levels(streams_of[2], (WALKERS,), ((0, 32),), -0.2, 0.2)), 0.04, 0.16)
    return dict(green=green, cholesky_rotated_vectors=cholesky_rotated_vectors, walker_weight=walker_weight)


def reference(green, cholesky_rotated_vectors, walker_weight):
    chol_float = cholesky_rotated_vectors.astype(jnp.float32)

    def one_walker(chol_sum, input_tuple):
        walker_green_matrix, weight = input_tuple
        green_float = walker_green_matrix.astype(jnp.float32)
        exchange_block = jnp.einsum("gim,jm->gij", chol_float, green_float)
        exchange_block = lax.optimization_barrier(exchange_block.astype(jnp.bfloat16)).astype(jnp.float32)
        green_term = -weight * jnp.einsum("gij,gjm->im", exchange_block, chol_float)
        chol_sum = chol_sum - weight * jnp.einsum("gji,jm->gim", exchange_block, green_float)
        return chol_sum, green_term

    zero_grad = jnp.zeros(cholesky_rotated_vectors.shape, jnp.float32)
    chol_sum, green_terms = lax.scan(one_walker, zero_grad, (green, walker_weight))
    return green_terms, chol_sum
```

```python
import functools

import jax
import jax.numpy as jnp
from jax import lax
from jax.experimental import pallas as pl
from jax.experimental.pallas import tpu as pltpu
from jax.sharding import PartitionSpec as P

MESH = pl.DeviceIdType.MESH
F32 = jnp.float32
BF16 = jnp.bfloat16
NT = (((1,), (1,)), ((), ()))
TN = (((0,), (0,)), ((), ()))


def each(count, body):
    if count <= 8:
        for step in range(count):
            body(step)
    else:
        lax.fori_loop(0, count, lambda step, _: (body(step), 0)[1], 0)


def kernel(
    depth, walk, weight_ref, green_ref, chol_ref, cot_ref, grad_ref,
    weight_tile, weights, greens, other, total, own_cot, cot_out, cot_in, grad_out, grad_in,
    green_sem, weight_sem, half_sem, mate_sem, cot_sem, grad_sem,
):
    me_c, me_k = lax.axis_index("chol"), lax.axis_index("walk")
    z, y = me_c // 2, me_c % 2
    pair = z * 2 + (1 - y)
    core = me_k % 2
    mate = me_k + 1 - 2 * core
    vectors, occupied, orbitals = chol_ref.shape
    half = vectors // 2
    rows = vectors * occupied
    part = orbitals // walk

    def up(step):
        return (((z + step) % depth) * 2 + y, me_k)

    def down(step):
        return (((z + depth - step) % depth) * 2 + y, me_k)

    def plane(index):
        return (z * 2 + (y + index // walk) % 2, (me_k + index % walk) % walk)

    barrier = pltpu.get_barrier_semaphore()

    def greet(device):
        pl.semaphore_signal(barrier, inc=1, device_id=device, device_id_type=MESH)

    each(depth - 1, lambda s: greet(up(s + 1)))
    for index in range(1, 2 * walk):
        greet(plane(index))
    pl.semaphore_wait(barrier, depth - 1 + 2 * walk - 1)

    def remote(src, dst, sems, index, device):
        return pltpu.make_async_remote_copy(
            src_ref=src, dst_ref=dst, send_sem=sems.at[0, index], recv_sem=sems.at[1, index],
            device_id=device, device_id_type=MESH,
        )

    def send_green(s):
        return remote(green_ref.at[0], greens.at[s], green_sem, s, up(s + 1))

    def send_weight(s):
        return remote(weight_tile, weights.at[s], weight_sem, s, up(s + 1))

    def send_cot(s):
        return remote(cot_out.at[s], cot_in.at[s], cot_sem, s, down(s + 1))

    def send_grad(index):
        return remote(
            grad_out.at[index - 1], grad_in.at[index - 1], grad_sem, index - 1, plane(index)
        )

    mine = pl.ds(core * half, half)
    send_half = remote(chol_ref.at[mine], other.at[mine], half_sem, 0, (pair, me_k))
    send_mate = remote(other.at[mine], other.at[mine], mate_sem, 0, (me_c, mate))

    send_half.start()
    each(depth - 1, lambda s: send_green(s).start())
    weight = weight_ref[0]
    weight_tile[...] = jnp.full(weight_tile.shape, weight, F32)
    each(depth - 1, lambda s: send_weight(s).start())

    def visit(walker, scale, vectors_ref, base, first):
        block = vectors_ref[...].reshape(rows, orbitals)
        swapped = lax.dot_general(block, walker, NT, preferred_element_type=F32).astype(BF16)
        pieces = [swapped[v * occupied:(v + 1) * occupied] for v in range(vectors)]
        cot = jnp.dot(jnp.concatenate(pieces, axis=1), block, preferred_element_type=F32)
        for v in range(vectors):
            term = scale * lax.dot_general(pieces[v], walker, TN, preferred_element_type=F32)
            at = pl.ds(base * rows + v * occupied, occupied)
            if first:
                total[at, :] = term
            else:
                total[at, :] += term
        return cot

    own_cot[...] = visit(green_ref[0], weight, chol_ref, 0, True)
    send_half.wait_recv()
    send_mate.start()
    send_mate.wait_recv()
    own_cot[...] += visit(green_ref[0], weight, other, 1, True)

    def visitor(s):
        send_green(s).wait_recv()
        send_weight(s).wait_recv()
        walker = greens[s]
        scale = weights[s][0:1, 0:1]
        cot = visit(walker, scale, chol_ref, 0, False) + visit(walker, scale, other, 1, False)
        cot_out[s] = cot.astype(BF16)
        send_cot(s).start()

    each(depth - 1, visitor)

    for index in range(1, 2 * walk):
        column = pl.multiple_of(((me_k + index % walk) % walk) * part, part)
        at = pl.ds((index // walk) * rows, rows)
        grad_out[index - 1] = total[at, pl.ds(column, part)].astype(BF16)
        send_grad(index).start()

    def add_cot(s):
        send_cot(s).wait_recv()
        own_cot[...] += cot_in[s].astype(F32)

    each(depth - 1, add_cot)
    cot_ref[0] = -weight * own_cot[...]
    grad = total[pl.ds(0, rows), pl.ds(pl.multiple_of(me_k * part, part), part)]
    for index in range(1, 2 * walk):
        send_grad(index).wait_recv()
        grad += grad_in[index - 1].astype(F32)
    grad_ref[...] = -grad.reshape(vectors, occupied, part)

    send_half.wait_send()
    send_mate.wait_send()
    for index in range(1, 2 * walk):
        send_grad(index).wait_send()

    def finish(s):
        send_green(s).wait_send()
        send_weight(s).wait_send()
        send_cot(s).wait_send()

    each(depth - 1, finish)


def shards(green, chol, weight):
    depth = lax.axis_size("chol") // 2
    walk = lax.axis_size("walk")
    vectors, occupied, orbitals = chol.shape
    rows = vectors * occupied
    part = orbitals // walk
    others = depth - 1
    vmem = pl.BlockSpec(memory_space=pltpu.VMEM)
    dma = pltpu.SemaphoreType.DMA
    return pl.pallas_call(
        functools.partial(kernel, depth, walk),
        out_shape=(
            jax.ShapeDtypeStruct((1, occupied, orbitals), F32),
            jax.ShapeDtypeStruct((vectors, occupied, part), F32),
        ),
        in_specs=[pl.BlockSpec(memory_space=pltpu.SMEM), vmem, vmem],
        out_specs=(vmem, vmem),
        scratch_shapes=[
            pltpu.VMEM((8, 128), F32),
            pltpu.VMEM((others, 8, 128), F32),
            pltpu.VMEM((others, occupied, orbitals), BF16),
            pltpu.VMEM((vectors, occupied, orbitals), BF16),
            pltpu.VMEM((2 * rows, orbitals), F32),
            pltpu.VMEM((occupied, orbitals), F32),
            pltpu.VMEM((others, occupied, orbitals), BF16),
            pltpu.VMEM((others, occupied, orbitals), BF16),
            pltpu.VMEM((2 * walk - 1, rows, part), BF16),
            pltpu.VMEM((2 * walk - 1, rows, part), BF16),
            dma((2, others)), dma((2, others)), dma((2, 1)), dma((2, 1)),
            dma((2, others)), dma((2, 2 * walk - 1)),
        ],
        compiler_params=pltpu.CompilerParams(
            collective_id=0, has_side_effects=True, vmem_limit_bytes=48 * 1024 * 1024
        ),
    )(weight, green, chol)


def solution(mesh):
    in_specs = (P(("chol", "walk"), None, None), P("chol", None, None), P(("chol", "walk")))
    out_specs = (P(("chol", "walk"), None, None), P("chol", None, "walk"))
    return jax.shard_map(shards, mesh=mesh, in_specs=in_specs, out_specs=out_specs, check_vma=False)
```

```python
import functools

import jax
import jax.numpy as jnp
from jax import lax
from jax.experimental import pallas as pl
from jax.experimental.pallas import tpu as pltpu
from jax.sharding import PartitionSpec as P

MESH = pl.DeviceIdType.MESH
F32 = jnp.float32
BF16 = jnp.bfloat16
NT = (((1,), (1,)), ((), ()))
TN = (((0,), (0,)), ((), ()))


def each(count, body):
    if count <= 8:
        for step in range(count):
            body(step)
    else:
        lax.fori_loop(0, count, lambda step, _: (body(step), 0)[1], 0)


def kernel(
    deep, wide, weight_ref, green_hbm, chol_hbm, cot_ref, grad_ref,
    green, chol, other, weight_tile, weights, near_green, hi_green, far_green,
    total, own_cot, near_part, hi_part, near_out, near_in, far_out, far_in, hi_out, hi_in,
    mate_out, mate_in, grad_out, grad_in,
    load_sem, half_sem, share_sem, near_sem, hi_sem, far_sem, weight_sem,
    near_cot_sem, far_cot_sem, hi_cot_sem, mate_sem, grad_sem,
):
    me_c, me_k = lax.axis_index("chol"), lax.axis_index("walk")
    hi, lo, y = me_c // 4, (me_c // 2) % 2, me_c % 2
    x, core = me_k // 2, me_k % 2
    vectors, occupied, orbitals = chol.shape
    half = vectors // 2
    rows = vectors * occupied
    part = orbitals // (2 * wide)
    steps = deep - 1

    def on_line(distance, flip):
        position = ((hi + distance) % deep) * 2 + (lo + flip) % 2
        return (position * 2 + y, me_k)

    def on_plane(flip, distance):
        return ((hi * 2 + lo) * 2 + (y + flip) % 2, ((x + distance) % wide) * 2 + core)

    near = on_line(0, 1)
    pair = on_plane(1, 0)
    mate = (me_c, x * 2 + (1 - core))
    units = [(flip, j) for flip in (1, 0) for j in reversed(range(wide))]

    loads = [
        pltpu.make_async_copy(green_hbm.at[0], green, load_sem.at[0]),
        pltpu.make_async_copy(chol_hbm, chol, load_sem.at[1]),
    ]
    for load in loads:
        load.start()

    barrier = pltpu.get_barrier_semaphore()

    def greet(device):
        pl.semaphore_signal(barrier, inc=1, device_id=device, device_id_type=MESH)

    greet(near)
    greet(mate)

    def greet_line(s):
        greet(on_line(s + 1, 0))
        greet(on_line(s + 1, 1))

    each(steps, greet_line)
    for flip, j in units[:-1]:
        greet(on_plane(flip, j))
    pl.semaphore_wait(barrier, 2 + 2 * steps + len(units) - 1)

    def remote(src, dst, sems, index, device):
        return pltpu.make_async_remote_copy(
            src_ref=src, dst_ref=dst, send_sem=sems.at[0, index], recv_sem=sems.at[1, index],
            device_id=device, device_id_type=MESH,
        )

    mine = pl.ds(core * half, half)
    send_half = remote(chol.at[mine], other.at[mine], half_sem, 0, pair)
    send_share = remote(other.at[mine], other.at[mine], share_sem, 0, mate)
    send_near = remote(green, near_green, near_sem, 0, near)
    send_near_weight = remote(weight_tile, weights.at[0], weight_sem, 0, near)
    send_near_cot = remote(near_out, near_in, near_cot_sem, 0, near)

    def send_hi(s):
        return remote(green, hi_green.at[s], hi_sem, s, on_line(s + 1, 0))

    def send_far(s):
        return remote(hi_green.at[s], far_green.at[s], far_sem, s, near)

    def send_weight(s, flip):
        slot = 1 + 2 * s + flip
        return remote(weight_tile, weights.at[slot], weight_sem, slot, on_line(s + 1, flip))

    def send_far_cot(s):
        return remote(far_out.at[s], far_in.at[s], far_cot_sem, s, near)

    def send_hi_cot(s):
        return remote(hi_out.at[s], hi_in.at[s], hi_cot_sem, s, on_line(deep - 1 - s, 0))

    def send_mate(u):
        return remote(mate_out.at[u], mate_in.at[u], mate_sem, u, mate)

    def send_grad(u):
        return remote(grad_out.at[u], grad_in.at[u], grad_sem, u, on_plane(*units[u]))

    loads[0].wait()
    send_near.start()
    each(steps, lambda s: send_hi(s).start())
    loads[1].wait()
    send_half.start()
    weight = weight_ref[0]
    weight_tile[...] = jnp.full(weight_tile.shape, weight, F32)
    send_near_weight.start()

    def start_weights(s):
        send_weight(s, 0).start()
        send_weight(s, 1).start()

    each(steps, start_weights)

    def visit(walker, scale, vectors_ref, base, first):
        block = vectors_ref[...].reshape(rows, orbitals)
        swapped = lax.dot_general(block, walker, NT, preferred_element_type=F32).astype(BF16)
        pieces = [swapped[v * occupied:(v + 1) * occupied] for v in range(vectors)]
        cot = jnp.dot(jnp.concatenate(pieces, axis=1), block, preferred_element_type=F32)
        for v in range(vectors):
            term = scale * lax.dot_general(pieces[v], walker, TN, preferred_element_type=F32)
            at = pl.ds(base * rows + v * occupied, occupied)
            if first:
                total[at, :] = term
            else:
                total[at, :] += term
        return cot

    def scale_of(slot):
        return weights[slot][0:1, 0:1]

    own_cot[...] = visit(green[...], weight, chol, 0, True)
    send_near.wait_recv()
    send_near_weight.wait_recv()
    near_part[...] = visit(near_green[...], scale_of(0), chol, 0, False)
    send_half.wait_recv()
    send_share.start()

    def meet_hi(s):
        send_hi(s).wait_recv()
        send_far(s).start()
        send_weight(s, 0).wait_recv()
        hi_part[s] = visit(hi_green[s], scale_of(1 + 2 * s), chol, 0, False)

    each(steps, meet_hi)
    send_share.wait_recv()
    cot = near_part[...] + visit(near_green[...], scale_of(0), other, 1, True)
    near_out[...] = cot.astype(BF16)
    send_near_cot.start()
    own_cot[...] += visit(green[...], weight, other, 1, False)

    def finish_hi(s):
        hi_part[s] += visit(hi_green[s], scale_of(1 + 2 * s), other, 1, False)

    each(steps, finish_hi)

    def meet_far(s):
        send_far(s).wait_recv()
        send_weight(s, 1).wait_recv()
        scale = scale_of(2 + 2 * s)
        cot = visit(far_green[s], scale, chol, 0, False)
        cot += visit(far_green[s], scale, other, 1, False)
        far_out[s] = cot.astype(BF16)
        send_far_cot(s).start()

    each(steps, meet_far)

    def piece(unit, of_core):
        flip, j = unit
        column = pl.multiple_of((((x + j) % wide) * 2 + of_core) * part, part)
        return total[pl.ds(flip * rows, rows), pl.ds(column, part)]

    for u, unit in enumerate(units):
        mate_out[u] = piece(unit, 1 - core).astype(BF16)
        send_mate(u).start()
    for u, unit in enumerate(units[:-1]):
        send_mate(u).wait_recv()
        grad_out[u] = (piece(unit, core) + mate_in[u].astype(F32)).astype(BF16)
        send_grad(u).start()

    def pass_hi(s):
        send_far_cot(s).wait_recv()
        hi_out[s] = (hi_part[s] + far_in[s].astype(F32)).astype(BF16)
        send_hi_cot(s).start()

    each(steps, pass_hi)

    last = len(units) - 1
    send_mate(last).wait_recv()
    grad = piece(units[last], core) + mate_in[last].astype(F32)
    for u in range(last):
        send_grad(u).wait_recv()
        grad += grad_in[u].astype(F32)
    grad_ref[...] = -grad.reshape(vectors, occupied, part)

    send_near_cot.wait_recv()
    own_cot[...] += near_in[...].astype(F32)

    def add_hi(s):
        send_hi_cot(s).wait_recv()
        own_cot[...] += hi_in[s].astype(F32)

    each(steps, add_hi)
    cot_ref[0] = -weight * own_cot[...]

    for copy in (send_half, send_share, send_near, send_near_weight, send_near_cot):
        copy.wait_send()

    def finish(s):
        for copy in (
            send_hi(s), send_far(s), send_weight(s, 0), send_weight(s, 1),
            send_far_cot(s), send_hi_cot(s),
        ):
            copy.wait_send()

    each(steps, finish)
    for u in range(len(units)):
        send_mate(u).wait_send()
    for u in range(last):
        send_grad(u).wait_send()


def shards(green, chol, weight):
    deep = lax.axis_size("chol") // 4
    wide = lax.axis_size("walk") // 2
    vectors, occupied, orbitals = chol.shape
    rows = vectors * occupied
    part = orbitals // (2 * wide)
    steps = deep - 1
    units = 2 * wide
    matrix = (occupied, orbitals)
    vmem = pl.BlockSpec(memory_space=pltpu.VMEM)
    anywhere = pl.BlockSpec(memory_space=pl.ANY)
    dma = pltpu.SemaphoreType.DMA
    return pl.pallas_call(
        functools.partial(kernel, deep, wide),
        out_shape=(
            jax.ShapeDtypeStruct((1, occupied, orbitals), F32),
            jax.ShapeDtypeStruct((vectors, occupied, part), F32),
        ),
        in_specs=[pl.BlockSpec(memory_space=pltpu.SMEM), anywhere, anywhere],
        out_specs=(vmem, vmem),
        scratch_shapes=[
            pltpu.VMEM(matrix, BF16),
            pltpu.VMEM((vectors,) + matrix, BF16),
            pltpu.VMEM((vectors,) + matrix, BF16),
            pltpu.VMEM((8, 128), F32),
            pltpu.VMEM((1 + 2 * steps, 8, 128), F32),
            pltpu.VMEM(matrix, BF16),
            pltpu.VMEM((steps,) + matrix, BF16),
            pltpu.VMEM((steps,) + matrix, BF16),
            pltpu.VMEM((2 * rows, orbitals), F32),
            pltpu.VMEM(matrix, F32),
            pltpu.VMEM(matrix, F32),
            pltpu.VMEM((steps,) + matrix, F32),
            pltpu.VMEM(matrix, BF16),
            pltpu.VMEM(matrix, BF16),
            pltpu.VMEM((steps,) + matrix, BF16),
            pltpu.VMEM((steps,) + matrix, BF16),
            pltpu.VMEM((steps,) + matrix, BF16),
            pltpu.VMEM((steps,) + matrix, BF16),
            pltpu.VMEM((units, rows, part), BF16),
            pltpu.VMEM((units, rows, part), BF16),
            pltpu.VMEM((units - 1, rows, part), BF16),
            pltpu.VMEM((units - 1, rows, part), BF16),
            dma((2,)), dma((2, 1)), dma((2, 1)), dma((2, 1)), dma((2, steps)), dma((2, steps)),
            dma((2, 1 + 2 * steps)), dma((2, 1)), dma((2, steps)), dma((2, steps)),
            dma((2, units)), dma((2, units - 1)),
        ],
        compiler_params=pltpu.CompilerParams(
            collective_id=0, has_side_effects=True, vmem_limit_bytes=60 * 1024 * 1024
        ),
    )(weight, green, chol)


def solution(mesh):
    in_specs = (P(("chol", "walk"), None, None), P("chol", None, None), P(("chol", "walk")))
    out_specs = (P(("chol", "walk"), None, None), P("chol", None, "walk"))
    return jax.shard_map(shards, mesh=mesh, in_specs=in_specs, out_specs=out_specs, check_vma=False)
```

```python
import functools

import jax
import jax.numpy as jnp
from jax import lax
from jax.experimental import pallas as pl
from jax.experimental.pallas import tpu as pltpu
from jax.sharding import PartitionSpec as P

MESH = pl.DeviceIdType.MESH
F32 = jnp.float32
BF16 = jnp.bfloat16
NT = (((1,), (1,)), ((), ()))
CHUNKS = 2
VMEM_BYTES = 60 * 1024 * 1024


def each(count, body):
    if count <= 8:
        for step in range(count):
            body(step)
    else:
        lax.fori_loop(0, count, lambda step, _: (body(step), 0)[1], 0)


def kernel(
    deep, wide, weight_ref, green_hbm, chol_hbm, cot_ref, grad_ref,
    walkers, block, weight_tile, weights, total, own_cot, hi_part,
    near_out, near_in, far_out, far_in, hi_out, hi_in,
    mate_out, mate_in, grad_out, grad_in,
    load_sem, half_sem, share_sem, near_sem, hi_sem, far_sem, weight_sem,
    near_cot_sem, far_cot_sem, hi_cot_sem, mate_sem, grad_sem,
):
    me_c, me_k = lax.axis_index("chol"), lax.axis_index("walk")
    hi, lo, y = me_c // 4, (me_c // 2) % 2, me_c % 2
    x, core = me_k // 2, me_k % 2
    occupied, orbitals = walkers.shape[1:]
    rows = block.shape[0] // 2
    vectors = rows // occupied
    half = rows // 2
    part = orbitals // (2 * wide)
    steps = deep - 1
    cut = occupied // CHUNKS

    def on_line(distance, flip):
        position = ((hi + distance) % deep) * 2 + (lo + flip) % 2
        return (position * 2 + y, me_k)

    def on_plane(flip, distance):
        return ((hi * 2 + lo) * 2 + (y + flip) % 2, ((x + distance) % wide) * 2 + core)

    near = on_line(0, 1)
    pair = on_plane(1, 0)
    mate = (me_c, x * 2 + (1 - core))
    units = [(flip, j) for flip in (1, 0) for j in reversed(range(wide))]

    load_green = pltpu.make_async_copy(green_hbm.at[0], walkers.at[0], load_sem.at[0])
    load_chol = [
        pltpu.make_async_copy(
            chol_hbm.at[v], block.at[pl.ds(v * occupied, occupied)], load_sem.at[1 + v]
        )
        for v in range(vectors)
    ]
    load_green.start()
    for load in load_chol:
        load.start()

    barrier = pltpu.get_barrier_semaphore()

    def greet(device):
        pl.semaphore_signal(barrier, inc=1, device_id=device, device_id_type=MESH)

    greet(near)
    greet(mate)

    def greet_line(s):
        greet(on_line(s + 1, 0))
        greet(on_line(s + 1, 1))

    each(steps, greet_line)
    for flip, j in units[:-1]:
        greet(on_plane(flip, j))
    weight = weight_ref[0]
    weight_tile[...] = jnp.full(weight_tile.shape, weight, F32)
    pl.semaphore_wait(barrier, 2 + 2 * steps + len(units) - 1)

    def remote(src, dst, sems, index, device):
        return pltpu.make_async_remote_copy(
            src_ref=src, dst_ref=dst, send_sem=sems.at[0, index], recv_sem=sems.at[1, index],
            device_id=device, device_id_type=MESH,
        )

    def send_half(p):
        size = half // CHUNKS
        src = pl.ds(pl.multiple_of(core * half + p * size, size), size)
        dst = pl.ds(pl.multiple_of(rows + core * half + p * size, size), size)
        return remote(block.at[src], block.at[dst], half_sem, p, pair)

    def send_share(p):
        size = half // CHUNKS
        at = pl.ds(pl.multiple_of(rows + core * half + p * size, size), size)
        return remote(block.at[at], block.at[at], share_sem, p, mate)

    send_near = remote(walkers.at[0], walkers.at[1], near_sem, 0, near)
    send_near_weight = remote(weight_tile, weights.at[0], weight_sem, 0, near)
    send_near_cot = remote(near_out, near_in, near_cot_sem, 0, near)

    def send_hi(s, p):
        at = pl.ds(p * cut, cut)
        return remote(
            walkers.at[0, at], walkers.at[2 + 2 * s, at], hi_sem, s * CHUNKS + p, on_line(s + 1, 0)
        )

    def send_far(s, p):
        at = pl.ds(p * cut, cut)
        return remote(
            walkers.at[2 + 2 * s, at], walkers.at[3 + 2 * s, at], far_sem, s * CHUNKS + p, near
        )

    def send_weight(s, flip):
        slot = 1 + 2 * s + flip
        return remote(weight_tile, weights.at[slot], weight_sem, slot, on_line(s + 1, flip))

    def send_far_cot(s, p):
        at = pl.ds(p * cut, cut)
        return remote(far_out.at[s, at], far_in.at[s, at], far_cot_sem, s * CHUNKS + p, near)

    def send_hi_cot(s, p):
        at = pl.ds(p * cut, cut)
        return remote(
            hi_out.at[s, at], hi_in.at[s, at], hi_cot_sem, s * CHUNKS + p, on_line(deep - 1 - s, 0)
        )

    def send_mate(u):
        return remote(mate_out.at[u], mate_in.at[u], mate_sem, u, mate)

    def send_grad(u):
        return remote(grad_out.at[u], grad_in.at[u], grad_sem, u, on_plane(*units[u]))

    load_green.wait()
    for p in range(CHUNKS):
        each(steps, lambda s: send_hi(s, p).start())
    send_near.start()
    for load in load_chol:
        load.wait()
    for p in range(CHUNKS):
        send_half(p).start()
    send_near_weight.start()

    def start_weights(s):
        send_weight(s, 0).start()
        send_weight(s, 1).start()

    each(steps, start_weights)

    def meet(first, count, base, size):
        held = block[pl.ds(base, size), :]
        stack = walkers[pl.ds(first, count)].reshape(count * occupied, orbitals)
        swapped = lax.dot_general(held, stack, NT, preferred_element_type=F32).astype(BF16)
        pieces = [
            [
                swapped[v * occupied:(v + 1) * occupied, w * occupied:(w + 1) * occupied]
                for v in range(size // occupied)
            ]
            for w in range(count)
        ]
        wide_rows = [jnp.concatenate(line, axis=1) for line in pieces]
        cots = jnp.dot(jnp.concatenate(wide_rows, axis=0), held, preferred_element_type=F32)
        return cots.reshape(count, occupied, orbitals), pieces

    def gradients(first, scales, base, size, pieces, fresh):
        term = None
        for w, scale in enumerate(scales):
            tall = jnp.concatenate([piece.T for piece in pieces[w]], axis=0)
            more = scale * jnp.dot(tall, walkers[first + w], preferred_element_type=F32)
            term = more if term is None else term + more
        at = pl.ds(base, size)
        if fresh:
            total[at, :] = term
        else:
            total[at, :] += term

    def scale_of(slot):
        return weights[slot][0:1, 0:1]

    send_near.wait_recv()
    send_near_weight.wait_recv()
    cots, pieces = meet(0, 2, 0, rows)
    own_cot[...] = cots
    gradients(0, [weight, scale_of(0)], 0, rows, pieces, True)

    for p in range(CHUNKS):
        def pass_green(s):
            send_hi(s, p).wait_recv()
            send_far(s, p).start()

        each(steps, pass_green)
        send_half(p).wait_recv()
        send_share(p).start()

    def meet_hi(s):
        send_weight(s, 0).wait_recv()
        cots, pieces = meet(2 + 2 * s, 1, 0, rows)
        hi_part[s] = cots[0]
        gradients(2 + 2 * s, [scale_of(1 + 2 * s)], 0, rows, pieces, False)

    each(steps, meet_hi)
    for p in range(CHUNKS):
        send_share(p).wait_recv()
    cots, pieces = meet(0, 2, rows, rows)
    own_cot[...] += cots
    near_out[...] = own_cot[1].astype(BF16)
    send_near_cot.start()
    gradients(0, [weight, scale_of(0)], rows, rows, pieces, True)

    def meet_far(s):
        for p in range(CHUNKS):
            send_far(s, p).wait_recv()
        send_weight(s, 1).wait_recv()
        cots, pieces = meet(3 + 2 * s, 1, 0, 2 * rows)
        far_out[s] = cots[0].astype(BF16)
        for p in range(CHUNKS):
            send_far_cot(s, p).start()
        gradients(3 + 2 * s, [scale_of(2 + 2 * s)], 0, 2 * rows, pieces, False)

    each(steps, meet_far)

    def finish_hi(s):
        cots, pieces = meet(2 + 2 * s, 1, rows, rows)
        hi_part[s] += cots[0]
        gradients(2 + 2 * s, [scale_of(1 + 2 * s)], rows, rows, pieces, False)

    each(steps, finish_hi)

    def piece_of(unit, of_core):
        flip, j = unit
        column = pl.multiple_of((((x + j) % wide) * 2 + of_core) * part, part)
        return total[pl.ds(flip * rows, rows), pl.ds(column, part)]

    for u, unit in enumerate(units):
        mate_out[u] = piece_of(unit, 1 - core).astype(BF16)
        send_mate(u).start()
    for u, unit in enumerate(units[:-1]):
        send_mate(u).wait_recv()
        grad_out[u] = (piece_of(unit, core) + mate_in[u].astype(F32)).astype(BF16)
        send_grad(u).start()

    for p in range(CHUNKS):
        at = pl.ds(p * cut, cut)

        def pass_cot(s):
            send_far_cot(s, p).wait_recv()
            hi_out[s, at] = (hi_part[s, at] + far_in[s, at].astype(F32)).astype(BF16)
            send_hi_cot(s, p).start()

        each(steps, pass_cot)

    last = len(units) - 1
    send_mate(last).wait_recv()
    grad = piece_of(units[last], core) + mate_in[last].astype(F32)
    send_near_cot.wait_recv()
    own_cot[0] += near_in[...].astype(F32)
    for u in range(last):
        send_grad(u).wait_recv()
        grad += grad_in[u].astype(F32)
    grad_ref[...] = -grad.reshape(vectors, occupied, part)

    def add_hi(s):
        for p in range(CHUNKS):
            send_hi_cot(s, p).wait_recv()
        own_cot[0] += hi_in[s].astype(F32)

    each(steps, add_hi)
    cot_ref[0] = -weight * own_cot[0]

    for copy in (send_near, send_near_weight, send_near_cot):
        copy.wait_send()
    for p in range(CHUNKS):
        send_half(p).wait_send()
        send_share(p).wait_send()

    def finish(s):
        send_weight(s, 0).wait_send()
        send_weight(s, 1).wait_send()
        for p in range(CHUNKS):
            for send in (send_hi, send_far, send_far_cot, send_hi_cot):
                send(s, p).wait_send()

    each(steps, finish)
    for u in range(len(units)):
        send_mate(u).wait_send()
    for u in range(last):
        send_grad(u).wait_send()


def shards(green, chol, weight):
    deep = lax.axis_size("chol") // 4
    wide = lax.axis_size("walk") // 2
    vectors, occupied, orbitals = chol.shape
    rows = vectors * occupied
    part = orbitals // (2 * wide)
    steps = deep - 1
    units = 2 * wide
    matrix = (occupied, orbitals)
    vmem = pl.BlockSpec(memory_space=pltpu.VMEM)
    anywhere = pl.BlockSpec(memory_space=pl.ANY)
    dma = pltpu.SemaphoreType.DMA
    return pl.pallas_call(
        functools.partial(kernel, deep, wide),
        out_shape=(
            jax.ShapeDtypeStruct((1, occupied, orbitals), F32),
            jax.ShapeDtypeStruct((vectors, occupied, part), F32),
        ),
        in_specs=[pl.BlockSpec(memory_space=pltpu.SMEM), anywhere, anywhere],
        out_specs=(vmem, vmem),
        scratch_shapes=[
            pltpu.VMEM((2 * deep,) + matrix, BF16),
            pltpu.VMEM((2 * rows, orbitals), BF16),
            pltpu.VMEM((8, 128), F32),
            pltpu.VMEM((1 + 2 * steps, 8, 128), F32),
            pltpu.VMEM((2 * rows, orbitals), F32),
            pltpu.VMEM((2,) + matrix, F32),
            pltpu.VMEM((steps,) + matrix, F32),
            pltpu.VMEM(matrix, BF16),
            pltpu.VMEM(matrix, BF16),
            pltpu.VMEM((steps,) + matrix, BF16),
            pltpu.VMEM((steps,) + matrix, BF16),
            pltpu.VMEM((steps,) + matrix, BF16),
            pltpu.VMEM((steps,) + matrix, BF16),
            pltpu.VMEM((units, rows, part), BF16),
            pltpu.VMEM((units, rows, part), BF16),
            pltpu.VMEM((units - 1, rows, part), BF16),
            pltpu.VMEM((units - 1, rows, part), BF16),
            dma((1 + vectors,)), dma((2, CHUNKS)), dma((2, CHUNKS)), dma((2, 1)),
            dma((2, steps * CHUNKS)), dma((2, steps * CHUNKS)),
            dma((2, 1 + 2 * steps)), dma((2, 1)),
            dma((2, steps * CHUNKS)), dma((2, steps * CHUNKS)),
            dma((2, units)), dma((2, units - 1)),
        ],
        compiler_params=pltpu.CompilerParams(
            collective_id=0, has_side_effects=True, vmem_limit_bytes=VMEM_BYTES
        ),
    )(weight, green, chol)


def solution(mesh):
    in_specs = (P(("chol", "walk"), None, None), P("chol", None, None), P(("chol", "walk")))
    out_specs = (P(("chol", "walk"), None, None), P("chol", None, "walk"))
    return jax.shard_map(shards, mesh=mesh, in_specs=in_specs, out_specs=out_specs, check_vma=False)
```

```python
import functools

import jax
import jax.numpy as jnp
from jax import lax
from jax.experimental import pallas as pl
from jax.experimental.pallas import tpu as pltpu
from jax.sharding import PartitionSpec as P

MESH = pl.DeviceIdType.MESH
F32 = jnp.float32
BF16 = jnp.bfloat16
NT = (((1,), (1,)), ((), ()))
CHUNKS = 2
VMEM_BYTES = 60 * 1024 * 1024


def each(count, body):
    if count <= 8:
        for step in range(count):
            body(step)
    else:
        lax.fori_loop(0, count, lambda step, _: (body(step), 0)[1], 0)


def at_least(a, b, bound):
    return (a - b + bound) // bound


def kernel(
    line, wide, weight_ref, green_hbm, chol_hbm, cot_ref, grad_ref,
    walkers, block, weight_tile, weights, total, own_cot, parts,
    cot_out, cot_in, mate_out, mate_in, grad_out, grad_in,
    load_sem, half_sem, share_sem, green_out_sem, green_in_sem, weight_sem,
    cot_out_sem, cot_in_sem, mate_sem, grad_sem,
):
    me_c, me_k = lax.axis_index("chol"), lax.axis_index("walk")
    z, y = me_c // 2, me_c % 2
    x, core = me_k // 2, me_k % 2
    occupied, orbitals = walkers.shape[1:]
    rows = block.shape[0] // 2
    vectors = rows // occupied
    half = rows // 2
    part = orbitals // (2 * wide)
    cut = occupied // CHUNKS
    bound = 4 * line
    lower = at_least(line - 1 - z, z, bound)
    outward = 2 * lower - 1
    short = lower * z + (1 - lower) * (line - 1 - z)

    def on_line(position):
        return (position * 2 + y, me_k)

    def on_plane(flip, distance):
        return (z * 2 + (y + flip) % 2, ((x + distance) % wide) * 2 + core)

    def inside(position):
        return (position >= 0) & (position < line)

    def arrival(s):
        near = at_least(2 * short, s, bound)
        distance = near * ((s + 1) // 2) + (1 - near) * (s - short)
        sign = near * (1 - 2 * (s % 2)) + (1 - near)
        return z + distance * sign * outward

    def passing(i):
        far = line - 1 - short
        first = at_least(far - 1, i, bound)
        return z + outward * (first * (1 + i) - (1 - first) * (1 + i - far))

    def above(w):
        return at_least(w, z + 1, bound)

    def beyond(w):
        return z + 1 - 2 * above(w)

    mate = (me_c, x * 2 + (1 - core))
    pair = on_plane(1, 0)
    units = [(flip, j) for flip in (1, 0) for j in reversed(range(wide))]

    load_green = pltpu.make_async_copy(green_hbm.at[0], walkers.at[z], load_sem.at[0])
    load_chol = [
        pltpu.make_async_copy(
            chol_hbm.at[v], block.at[pl.ds(v * occupied, occupied)], load_sem.at[1 + v]
        )
        for v in range(vectors)
    ]
    load_green.start()
    for load in load_chol:
        load.start()

    barrier = pltpu.get_barrier_semaphore()

    def greet(device):
        pl.semaphore_signal(barrier, inc=1, device_id=device, device_id_type=MESH)

    greet(mate)
    each(line - 1, lambda s: greet(on_line((z + s + 1) % line)))
    for flip, j in units[:-1]:
        greet(on_plane(flip, j))
    weight = weight_ref[0]
    weight_tile[...] = jnp.full(weight_tile.shape, weight, F32)
    pl.semaphore_wait(barrier, 1 + line - 1 + len(units) - 1)

    def remote(src, dst, send_sem, recv_sem, device):
        return pltpu.make_async_remote_copy(
            src_ref=src, dst_ref=dst, send_sem=send_sem, recv_sem=recv_sem,
            device_id=device, device_id_type=MESH,
        )

    def send_half(p):
        size = half // CHUNKS
        src = pl.ds(pl.multiple_of(core * half + p * size, size), size)
        dst = pl.ds(pl.multiple_of(rows + core * half + p * size, size), size)
        return remote(block.at[src], block.at[dst], half_sem.at[0, p], half_sem.at[1, p], pair)

    def send_share(p):
        size = half // CHUNKS
        at = pl.ds(pl.multiple_of(rows + core * half + p * size, size), size)
        return remote(block.at[at], block.at[at], share_sem.at[0, p], share_sem.at[1, p], mate)

    def send_green(w, p, position, slot):
        at = pl.ds(p * cut, cut)
        return remote(
            walkers.at[w, at], walkers.at[w, at],
            green_out_sem.at[slot * CHUNKS + p], green_in_sem.at[w * CHUNKS + p], on_line(position),
        )

    def send_weight(s):
        return remote(
            weight_tile, weights.at[z], weight_sem.at[0, s], weight_sem.at[1, z],
            on_line((z + s + 1) % line),
        )

    def wait_weight(w):
        remote(
            weight_tile, weights.at[w], weight_sem.at[0, 0], weight_sem.at[1, w], mate
        ).wait_recv()

    def send_cot(w, p):
        at = pl.ds(p * cut, cut)
        side = above(w)
        return remote(
            cot_out.at[w, at], cot_in.at[side, w, at], cot_out_sem.at[w * CHUNKS + p],
            cot_in_sem.at[side, w * CHUNKS + p], on_line(z - 1 + 2 * side),
        )

    def wait_cot(w, p, side):
        at = pl.ds(p * cut, cut)
        remote(
            cot_out.at[w, at], cot_in.at[side, w, at], cot_out_sem.at[w * CHUNKS + p],
            cot_in_sem.at[side, w * CHUNKS + p], mate,
        ).wait_recv()

    def send_mate(u):
        return remote(mate_out.at[u], mate_in.at[u], mate_sem.at[0, u], mate_sem.at[1, u], mate)

    def send_grad(u):
        return remote(
            grad_out.at[u], grad_in.at[u], grad_sem.at[0, u], grad_sem.at[1, u],
            on_plane(*units[u]),
        )

    ends = ((z + 1, z), (z - 1, line))

    load_green.wait()
    for p in range(CHUNKS):
        for position, slot in ends:
            @pl.when(inside(position))
            def _():
                send_green(z, p, position, slot).start()

    for load in load_chol:
        load.wait()
    for p in range(CHUNKS):
        send_half(p).start()
    each(line - 1, lambda s: send_weight(s).start())

    def meet(names, base, size):
        held = block[pl.ds(base, size), :]
        stack = jnp.concatenate([walkers[w] for w in names], axis=0)
        swapped = lax.dot_general(held, stack, NT, preferred_element_type=F32).astype(BF16)
        pieces = [
            [
                swapped[v * occupied:(v + 1) * occupied, n * occupied:(n + 1) * occupied]
                for v in range(size // occupied)
            ]
            for n in range(len(names))
        ]
        wide_rows = [jnp.concatenate(row, axis=1) for row in pieces]
        cots = jnp.dot(jnp.concatenate(wide_rows, axis=0), held, preferred_element_type=F32)
        return [cots[n * occupied:(n + 1) * occupied] for n in range(len(names))], pieces

    def gradients(names, scales, base, size, pieces, fresh):
        term = None
        for w, scale, row in zip(names, scales, pieces):
            tall = jnp.concatenate([piece.T for piece in row], axis=0)
            more = scale * jnp.dot(tall, walkers[w], preferred_element_type=F32)
            term = more if term is None else term + more
        at = pl.ds(base, size)
        if fresh:
            total[at, :] = term
        else:
            total[at, :] += term

    def take(w):
        for p in range(CHUNKS):
            send_green(w, p, z, w).wait_recv()

            @pl.when(inside(beyond(w)))
            def _():
                send_green(w, p, beyond(w), w).start()

        wait_weight(w)
        return weights[w][0:1, 0:1]

    def give(w, cot):
        parts[w] = cot

        @pl.when(jnp.logical_not(inside(beyond(w))))
        def _():
            cot_out[w] = cot.astype(BF16)
            for p in range(CHUNKS):
                send_cot(w, p).start()

    first = arrival(1)
    scale = take(first)
    cots, pieces = meet([z, first], 0, rows)
    own_cot[...] = cots[0]
    parts[first] = cots[1]
    gradients([z, first], [weight, scale], 0, rows, pieces, True)
    for p in range(CHUNKS):
        send_half(p).wait_recv()
        send_share(p).start()
    if line > 2:
        second = arrival(2)
        scale_second = take(second)
        cots, pieces = meet([second], 0, rows)
        parts[second] = cots[0]
        gradients([second], [scale_second], 0, rows, pieces, False)
    for p in range(CHUNKS):
        send_share(p).wait_recv()
    cots, pieces = meet([z, first], rows, rows)
    own_cot[...] += cots[0]
    give(first, parts[first] + cots[1])
    gradients([z, first], [weight, scale], rows, rows, pieces, True)
    if line > 2:
        cots, pieces = meet([second], rows, rows)
        give(second, parts[second] + cots[0])
        gradients([second], [scale_second], rows, rows, pieces, False)

    def later(s):
        w = arrival(s + 3)
        scale = take(w)
        cots, pieces = meet([w], 0, 2 * rows)
        give(w, cots[0])
        gradients([w], [scale], 0, 2 * rows, pieces, False)

    each(max(line - 3, 0), later)

    def piece_of(unit, of_core):
        flip, j = unit
        column = pl.multiple_of((((x + j) % wide) * 2 + of_core) * part, part)
        return total[pl.ds(flip * rows, rows), pl.ds(column, part)]

    def pass_cot(i):
        w = passing(i)

        @pl.when(inside(beyond(w)))
        def _():
            for p in range(CHUNKS):
                at = pl.ds(p * cut, cut)
                wait_cot(w, p, above(w))
                cot = parts[w, at] + cot_in[above(w), w, at].astype(F32)
                cot_out[w, at] = cot.astype(BF16)
                send_cot(w, p).start()

    for u, unit in enumerate(units):
        mate_out[u] = piece_of(unit, 1 - core).astype(BF16)
        send_mate(u).start()
    pass_cot(0)
    for u, unit in enumerate(units[:-1]):
        send_mate(u).wait_recv()
        grad_out[u] = (piece_of(unit, core) + mate_in[u].astype(F32)).astype(BF16)
        send_grad(u).start()
    each(line - 2, lambda i: pass_cot(i + 1))

    last = len(units) - 1
    send_mate(last).wait_recv()
    grad = piece_of(units[last], core) + mate_in[last].astype(F32)
    for u in range(last):
        send_grad(u).wait_recv()
        grad += grad_in[u].astype(F32)
    grad_ref[...] = -grad.reshape(vectors, occupied, part)

    for side, position in ((1, z - 1), (0, z + 1)):
        @pl.when(inside(position))
        def _():
            for p in range(CHUNKS):
                at = pl.ds(p * cut, cut)
                wait_cot(z, p, side)
                own_cot[at, :] += cot_in[side, z, at].astype(F32)

    cot_ref[0] = -weight * own_cot[...]

    for p in range(CHUNKS):
        send_half(p).wait_send()
        send_share(p).wait_send()
        for position, slot in ends:
            @pl.when(inside(position))
            def _():
                send_green(z, p, position, slot).wait_send()

    def finish(s):
        send_weight(s).wait_send()
        w = arrival(s + 1)
        for p in range(CHUNKS):
            send_cot(w, p).wait_send()

            @pl.when(inside(beyond(w)))
            def _():
                send_green(w, p, beyond(w), w).wait_send()

    each(line - 1, finish)
    for u in range(len(units)):
        send_mate(u).wait_send()
    for u in range(last):
        send_grad(u).wait_send()


def hand_over(cot, grad, cot_out, grad_out, sems):
    copies = []
    for v in range(grad.shape[0]):
        copies.append(pltpu.make_async_copy(grad.at[v], grad_out.at[v], sems.at[0, v]))
        size = cot.shape[1] // grad.shape[0]
        at = pl.ds(v * size, size)
        copies.append(pltpu.make_async_copy(cot.at[0, at], cot_out.at[0, at], sems.at[1, v]))
    for copy in copies:
        copy.start()
    for copy in copies:
        copy.wait()


def shards(green, chol, weight):
    line = lax.axis_size("chol") // 2
    wide = lax.axis_size("walk") // 2
    vectors, occupied, orbitals = chol.shape
    rows = vectors * occupied
    part = orbitals // (2 * wide)
    units = 2 * wide
    matrix = (occupied, orbitals)
    vmem = pl.BlockSpec(memory_space=pltpu.VMEM)
    anywhere = pl.BlockSpec(memory_space=pl.ANY)
    dma = pltpu.SemaphoreType.DMA
    out_shape = (
        jax.ShapeDtypeStruct((1, occupied, orbitals), F32),
        jax.ShapeDtypeStruct((vectors, occupied, part), F32),
    )
    cot, grad = pl.pallas_call(
        functools.partial(kernel, line, wide),
        out_shape=out_shape,
        in_specs=[pl.BlockSpec(memory_space=pltpu.SMEM), anywhere, anywhere],
        out_specs=(vmem, vmem),
        scratch_shapes=[
            pltpu.VMEM((line,) + matrix, BF16),
            pltpu.VMEM((2 * rows, orbitals), BF16),
            pltpu.VMEM((8, 128), F32),
            pltpu.VMEM((line, 8, 128), F32),
            pltpu.VMEM((2 * rows, orbitals), F32),
            pltpu.VMEM(matrix, F32),
            pltpu.VMEM((line,) + matrix, F32),
            pltpu.VMEM((line,) + matrix, BF16),
            pltpu.VMEM((2, line) + matrix, BF16),
            pltpu.VMEM((units, rows, part), BF16),
            pltpu.VMEM((units, rows, part), BF16),
            pltpu.VMEM((units - 1, rows, part), BF16),
            pltpu.VMEM((units - 1, rows, part), BF16),
            dma((1 + vectors,)), dma((2, CHUNKS)), dma((2, CHUNKS)),
            dma(((line + 1) * CHUNKS,)), dma((line * CHUNKS,)), dma((2, line)),
            dma((line * CHUNKS,)), dma((2, line * CHUNKS)),
            dma((2, units)), dma((2, units - 1)),
        ],
        compiler_params=pltpu.CompilerParams(
            collective_id=0, has_side_effects=True, vmem_limit_bytes=VMEM_BYTES
        ),
    )(weight, green, chol)
    return pl.pallas_call(
        hand_over,
        out_shape=out_shape,
        in_specs=[anywhere, anywhere],
        out_specs=(anywhere, anywhere),
        scratch_shapes=[dma((2, vectors))],
        compiler_params=pltpu.CompilerParams(vmem_limit_bytes=VMEM_BYTES),
    )(cot, grad)


def solution(mesh):
    in_specs = (P(("chol", "walk"), None, None), P("chol", None, None), P(("chol", "walk")))
    out_specs = (P(("chol", "walk"), None, None), P("chol", None, "walk"))
    return jax.shard_map(shards, mesh=mesh, in_specs=in_specs, out_specs=out_specs, check_vma=False)
```

```python
import functools

import jax
import jax.numpy as jnp
from jax import lax
from jax.experimental import pallas as pl
from jax.experimental.pallas import tpu as pltpu
from jax.sharding import PartitionSpec as P

MESH = pl.DeviceIdType.MESH
F32 = jnp.float32
BF16 = jnp.bfloat16
NT = (((1,), (1,)), ((), ()))
CHUNKS = 2
VMEM_BYTES = 60 * 1024 * 1024


def each(count, body):
    if count <= 8:
        for step in range(count):
            body(step)
    else:
        lax.fori_loop(0, count, lambda step, _: (body(step), 0)[1], 0)


def kernel(
    deep, wide, weight_ref, green_hbm, chol_hbm, cot_ref, grad_ref,
    walkers, block, weight_tile, weights, total, early_cot,
    near_out, near_in, far_out, far_in, hi_out, hi_in,
    mate_out, mate_in, grad_out, grad_in,
    load_sem, half_sem, share_sem, near_sem, hi_sem, far_sem, weight_sem,
    near_cot_sem, far_cot_sem, hi_cot_sem, mate_sem, grad_sem,
):
    me_c, me_k = lax.axis_index("chol"), lax.axis_index("walk")
    hi, lo, y = me_c // 4, (me_c // 2) % 2, me_c % 2
    x, core = me_k // 2, me_k % 2
    occupied, orbitals = walkers.shape[1:]
    rows = block.shape[0] // 2
    vectors = rows // occupied
    share = rows // (2 * CHUNKS)
    part = orbitals // (2 * wide)
    steps = deep - 1
    far = 2 + steps
    cut = occupied // CHUNKS

    def on_line(distance, flip):
        position = ((hi + distance) % deep) * 2 + (lo + flip) % 2
        return (position * 2 + y, me_k)

    def on_plane(flip, distance):
        return ((hi * 2 + lo) * 2 + (y + flip) % 2, ((x + distance) % wide) * 2 + core)

    near = on_line(0, 1)
    pair = on_plane(1, 0)
    mate = (me_c, x * 2 + (1 - core))
    units = [(flip, j) for flip in (1, 0) for j in reversed(range(wide))]

    load_green = pltpu.make_async_copy(green_hbm.at[0], walkers.at[0], load_sem.at[0])
    load_chol = [
        pltpu.make_async_copy(
            chol_hbm.at[v], block.at[pl.ds(v * occupied, occupied)], load_sem.at[1 + v]
        )
        for v in range(vectors)
    ]
    load_green.start()
    for load in load_chol:
        load.start()

    barrier = pltpu.get_barrier_semaphore()

    def greet(device):
        pl.semaphore_signal(barrier, inc=1, device_id=device, device_id_type=MESH)

    greet(near)
    greet(mate)

    def greet_line(s):
        greet(on_line(s + 1, 0))
        greet(on_line(s + 1, 1))

    each(steps, greet_line)
    for flip, j in units[:-1]:
        greet(on_plane(flip, j))
    weight = weight_ref[0]
    weight_tile[...] = jnp.full(weight_tile.shape, weight, F32)
    pl.semaphore_wait(barrier, 2 + 2 * steps + len(units) - 1)

    def remote(src, dst, sems, index, device):
        return pltpu.make_async_remote_copy(
            src_ref=src, dst_ref=dst, send_sem=sems.at[0, index], recv_sem=sems.at[1, index],
            device_id=device, device_id_type=MESH,
        )

    def send_half(p):
        start = (2 * p + core) * share
        src = pl.ds(pl.multiple_of(start, share), share)
        dst = pl.ds(pl.multiple_of(rows + start, share), share)
        return remote(block.at[src], block.at[dst], half_sem, p, pair)

    def send_share(p):
        at = pl.ds(pl.multiple_of(rows + (2 * p + core) * share, share), share)
        return remote(block.at[at], block.at[at], share_sem, p, mate)

    send_near = remote(walkers.at[0], walkers.at[1], near_sem, 0, near)
    send_near_weight = remote(weight_tile, weights.at[0], weight_sem, 0, near)
    send_near_cot = remote(near_out, near_in, near_cot_sem, 0, near)

    def send_hi(s, p):
        at = pl.ds(p * cut, cut)
        return remote(
            walkers.at[0, at], walkers.at[2 + s, at], hi_sem, s * CHUNKS + p, on_line(s + 1, 0)
        )

    def send_far(s, p):
        at = pl.ds(p * cut, cut)
        return remote(
            walkers.at[2 + s, at], walkers.at[far + s, at], far_sem, s * CHUNKS + p, near
        )

    def send_weight(s, flip):
        slot = 1 + s + flip * steps
        return remote(weight_tile, weights.at[slot], weight_sem, slot, on_line(s + 1, flip))

    def send_far_cot(s, p):
        at = pl.ds(p * cut, cut)
        return remote(far_out.at[s, at], far_in.at[s, at], far_cot_sem, s * CHUNKS + p, near)

    def send_hi_cot(s, p):
        at = pl.ds(p * cut, cut)
        return remote(
            hi_out.at[s, at], hi_in.at[s, at], hi_cot_sem, s * CHUNKS + p, on_line(deep - 1 - s, 0)
        )

    def send_mate(u):
        return remote(mate_out.at[u], mate_in.at[u], mate_sem, u, mate)

    def send_grad(u):
        return remote(grad_out.at[u], grad_in.at[u], grad_sem, u, on_plane(*units[u]))

    load_green.wait()
    for p in range(CHUNKS):
        each(steps, lambda s: send_hi(s, p).start())
    send_near.start()
    for load in load_chol:
        load.wait()
    for p in range(CHUNKS):
        send_half(p).start()
    send_near_weight.start()

    def start_weights(s):
        send_weight(s, 0).start()
        send_weight(s, 1).start()

    each(steps, start_weights)

    def meet(first, count, base, size):
        held = block[pl.ds(base, size), :]
        stack = walkers[pl.ds(first, count)].reshape(count * occupied, orbitals)
        swapped = lax.dot_general(held, stack, NT, preferred_element_type=F32).astype(BF16)
        pieces = [
            [
                swapped[v * occupied:(v + 1) * occupied, w * occupied:(w + 1) * occupied]
                for v in range(size // occupied)
            ]
            for w in range(count)
        ]
        wide_rows = [jnp.concatenate(line, axis=1) for line in pieces]
        cots = jnp.dot(jnp.concatenate(wide_rows, axis=0), held, preferred_element_type=F32)
        return cots.reshape(count, occupied, orbitals), pieces

    def gradients(first, scales, base, size, pieces, fresh):
        term = None
        for w, scale in enumerate(scales):
            tall = jnp.concatenate([piece.T for piece in pieces[w]], axis=0)
            more = scale * jnp.dot(tall, walkers[first + w], preferred_element_type=F32)
            term = more if term is None else term + more
        at = pl.ds(base, size)
        if fresh:
            total[at, :] = term
        else:
            total[at, :] += term

    def scale_of(slot):
        return weights[slot][0:1, 0:1]

    send_near.wait_recv()
    send_near_weight.wait_recv()
    cots, pieces = meet(0, 2, 0, rows)
    early_cot[0:2] = cots
    gradients(0, [weight, scale_of(0)], 0, rows, pieces, True)

    for p in range(CHUNKS):
        def pass_green(s):
            send_hi(s, p).wait_recv()
            send_far(s, p).start()

        each(steps, pass_green)
        send_half(p).wait_recv()
        send_share(p).start()

    def meet_hi(s):
        send_weight(s, 0).wait_recv()
        cots, pieces = meet(2 + s, 1, 0, rows)
        early_cot[2 + s] = cots[0]
        gradients(2 + s, [scale_of(1 + s)], 0, rows, pieces, False)

    each(steps, meet_hi)
    group = min(far, 3)
    scales = [weight] + [scale_of(w) for w in range(group - 1)]
    for p in range(CHUNKS):
        send_share(p).wait_recv()
        base = rows + 2 * p * share
        cots, pieces = meet(0, group, base, 2 * share)
        early_cot[0:group] += cots
        if p == CHUNKS - 1:
            near_out[...] = early_cot[1].astype(BF16)
            send_near_cot.start()
        gradients(0, scales, base, 2 * share, pieces, True)

        def finish_hi(s):
            cots, pieces = meet(group + s, 1, base, 2 * share)
            early_cot[group + s] += cots[0]
            gradients(group + s, [scale_of(group + s - 1)], base, 2 * share, pieces, False)

        each(far - group, finish_hi)

    def piece_of(unit, of_core):
        flip, j = unit
        column = pl.multiple_of((((x + j) % wide) * 2 + of_core) * part, part)
        return total[pl.ds(flip * rows, rows), pl.ds(column, part)]

    def meet_far(s, last):
        for p in range(CHUNKS):
            send_far(s, p).wait_recv()
        send_weight(s, 1).wait_recv()
        cots, pieces = meet(far + s, 1, 0, 2 * rows)
        far_out[s] = cots[0].astype(BF16)
        for p in range(CHUNKS):
            send_far_cot(s, p).start()
        for flip in (1, 0):
            chosen = [pieces[0][flip * vectors:(flip + 1) * vectors]]
            gradients(far + s, [scale_of(far - 1 + s)], flip * rows, rows, chosen, False)
            if last:
                for u, unit in enumerate(units):
                    if unit[0] == flip:
                        mate_out[u] = piece_of(unit, 1 - core).astype(BF16)
                        send_mate(u).start()

    each(steps - 1, lambda s: meet_far(s, False))
    meet_far(steps - 1, True)

    for u, unit in enumerate(units[:-1]):
        send_mate(u).wait_recv()
        grad_out[u] = (piece_of(unit, core) + mate_in[u].astype(F32)).astype(BF16)
        send_grad(u).start()

    for p in range(CHUNKS):
        at = pl.ds(p * cut, cut)

        def pass_cot(s):
            send_far_cot(s, p).wait_recv()
            hi_out[s, at] = (early_cot[2 + s, at] + far_in[s, at].astype(F32)).astype(BF16)
            send_hi_cot(s, p).start()

        each(steps, pass_cot)

    last = len(units) - 1
    send_mate(last).wait_recv()
    grad = piece_of(units[last], core) + mate_in[last].astype(F32)
    send_near_cot.wait_recv()
    early_cot[0] += near_in[...].astype(F32)
    for u in range(last):
        send_grad(u).wait_recv()
        grad += grad_in[u].astype(F32)
    grad_ref[...] = grad.reshape(vectors, occupied, part)

    def add_hi(s):
        for p in range(CHUNKS):
            send_hi_cot(s, p).wait_recv()
        early_cot[0] += hi_in[s].astype(F32)

    each(steps, add_hi)
    cot_ref[0] = weight * early_cot[0]

    for copy in (send_near, send_near_weight, send_near_cot):
        copy.wait_send()
    for p in range(CHUNKS):
        send_half(p).wait_send()
        send_share(p).wait_send()

    def finish(s):
        send_weight(s, 0).wait_send()
        send_weight(s, 1).wait_send()
        for p in range(CHUNKS):
            for send in (send_hi, send_far, send_far_cot, send_hi_cot):
                send(s, p).wait_send()

    each(steps, finish)
    for u in range(len(units)):
        send_mate(u).wait_send()
    for u in range(last):
        send_grad(u).wait_send()


def hand_over(cot, grad, cot_out, grad_out):
    cot_out[...] = -cot[...]
    grad_out[...] = -grad[...]


def shards(green, chol, weight):
    deep = lax.axis_size("chol") // 4
    wide = lax.axis_size("walk") // 2
    vectors, occupied, orbitals = chol.shape
    rows = vectors * occupied
    part = orbitals // (2 * wide)
    steps = deep - 1
    units = 2 * wide
    matrix = (occupied, orbitals)
    vmem = pl.BlockSpec(memory_space=pltpu.VMEM)
    anywhere = pl.BlockSpec(memory_space=pl.ANY)
    dma = pltpu.SemaphoreType.DMA
    out_shape = (
        jax.ShapeDtypeStruct((1, occupied, orbitals), F32),
        jax.ShapeDtypeStruct((vectors, occupied, part), F32),
    )
    cot, grad = pl.pallas_call(
        functools.partial(kernel, deep, wide),
        out_shape=out_shape,
        in_specs=[pl.BlockSpec(memory_space=pltpu.SMEM), anywhere, anywhere],
        out_specs=(vmem, vmem),
        scratch_shapes=[
            pltpu.VMEM((2 * deep,) + matrix, BF16),
            pltpu.VMEM((2 * rows, orbitals), BF16),
            pltpu.VMEM((8, 128), F32),
            pltpu.VMEM((1 + 2 * steps, 8, 128), F32),
            pltpu.VMEM((2 * rows, orbitals), F32),
            pltpu.VMEM((2 + steps,) + matrix, F32),
            pltpu.VMEM(matrix, BF16),
            pltpu.VMEM(matrix, BF16),
            pltpu.VMEM((steps,) + matrix, BF16),
            pltpu.VMEM((steps,) + matrix, BF16),
            pltpu.VMEM((steps,) + matrix, BF16),
            pltpu.VMEM((steps,) + matrix, BF16),
            pltpu.VMEM((units, rows, part), BF16),
            pltpu.VMEM((units, rows, part), BF16),
            pltpu.VMEM((units - 1, rows, part), BF16),
            pltpu.VMEM((units - 1, rows, part), BF16),
            dma((1 + vectors,)), dma((2, CHUNKS)), dma((2, CHUNKS)), dma((2, 1)),
            dma((2, steps * CHUNKS)), dma((2, steps * CHUNKS)),
            dma((2, 1 + 2 * steps)), dma((2, 1)),
            dma((2, steps * CHUNKS)), dma((2, steps * CHUNKS)),
            dma((2, units)), dma((2, units - 1)),
        ],
        compiler_params=pltpu.CompilerParams(
            collective_id=0, has_side_effects=True, vmem_limit_bytes=VMEM_BYTES
        ),
    )(weight, green, chol)
    return pl.pallas_call(
        hand_over,
        out_shape=out_shape,
        in_specs=[vmem, vmem],
        out_specs=(vmem, vmem),
        compiler_params=pltpu.CompilerParams(vmem_limit_bytes=VMEM_BYTES),
    )(cot, grad)


def solution(mesh):
    in_specs = (P(("chol", "walk"), None, None), P("chol", None, None), P(("chol", "walk")))
    out_specs = (P(("chol", "walk"), None, None), P("chol", None, "walk"))
    return jax.shard_map(shards, mesh=mesh, in_specs=in_specs, out_specs=out_specs, check_vma=False)
```

```python
import functools

import jax
import jax.numpy as jnp
from jax import lax
from jax.experimental import pallas as pl
from jax.experimental.pallas import tpu as pltpu
from jax.sharding import PartitionSpec as P

MESH = pl.DeviceIdType.MESH
F32 = jnp.float32
BF16 = jnp.bfloat16
NT = (((1,), (1,)), ((), ()))
CHUNKS = 2
VMEM_BYTES = 60 * 1024 * 1024


def each(count, body):
    if count <= 8:
        for step in range(count):
            body(step)
    else:
        lax.fori_loop(0, count, lambda step, _: (body(step), 0)[1], 0)


def kernel(
    deep, wide, weight_ref, green_hbm, chol_hbm, cot_ref, grad_ref,
    walkers, block, weight_tile, weights, total, early_cot,
    near_out, near_in, far_out, far_in, hi_out, hi_in,
    mate_out, mate_in, grad_out, grad_in,
    load_sem, half_sem, share_sem, near_sem, hi_sem, far_sem, weight_sem,
    near_cot_sem, far_cot_sem, hi_cot_sem, mate_sem, grad_sem,
):
    me_c, me_k = lax.axis_index("chol"), lax.axis_index("walk")
    hi, lo, y = me_c // 4, (me_c // 2) % 2, me_c % 2
    x, core = me_k // 2, me_k % 2
    occupied, orbitals = walkers.shape[1:]
    rows = block.shape[0] // 2
    vectors = rows // occupied
    share = rows // (2 * CHUNKS)
    part = orbitals // (2 * wide)
    steps = deep - 1
    far = 2 + steps
    cut = occupied // CHUNKS

    def on_line(distance, flip):
        position = ((hi + distance) % deep) * 2 + (lo + flip) % 2
        return (position * 2 + y, me_k)

    def on_plane(flip, distance):
        return ((hi * 2 + lo) * 2 + (y + flip) % 2, ((x + distance) % wide) * 2 + core)

    near = on_line(0, 1)
    pair = on_plane(1, 0)
    mate = (me_c, x * 2 + (1 - core))
    units = [(flip, j) for flip in (1, 0) for j in reversed(range(wide))]

    load_green = pltpu.make_async_copy(green_hbm.at[0], walkers.at[0], load_sem.at[0])
    load_chol = [
        pltpu.make_async_copy(
            chol_hbm.at[v], block.at[pl.ds(v * occupied, occupied)], load_sem.at[1 + v]
        )
        for v in range(vectors)
    ]
    load_green.start()
    for load in load_chol:
        load.start()

    barrier = pltpu.get_barrier_semaphore()

    def greet(device):
        pl.semaphore_signal(barrier, inc=1, device_id=device, device_id_type=MESH)

    greet(near)
    greet(mate)

    def greet_line(s):
        greet(on_line(s + 1, 0))
        greet(on_line(s + 1, 1))

    each(steps, greet_line)
    for flip, j in units[:-1]:
        greet(on_plane(flip, j))
    weight = weight_ref[0]
    weight_tile[...] = jnp.full(weight_tile.shape, weight, F32)
    pl.semaphore_wait(barrier, 2 + 2 * steps + len(units) - 1)

    def remote(src, dst, sems, index, device):
        return pltpu.make_async_remote_copy(
            src_ref=src, dst_ref=dst, send_sem=sems.at[0, index], recv_sem=sems.at[1, index],
            device_id=device, device_id_type=MESH,
        )

    def send_half(p):
        start = (2 * p + core) * share
        src = pl.ds(pl.multiple_of(start, share), share)
        dst = pl.ds(pl.multiple_of(rows + start, share), share)
        return remote(block.at[src], block.at[dst], half_sem, p, pair)

    def send_share(p):
        at = pl.ds(pl.multiple_of(rows + (2 * p + core) * share, share), share)
        return remote(block.at[at], block.at[at], share_sem, p, mate)

    send_near = remote(walkers.at[0], walkers.at[1], near_sem, 0, near)
    send_near_weight = remote(weight_tile, weights.at[0], weight_sem, 0, near)
    send_near_cot = remote(near_out, near_in, near_cot_sem, 0, near)

    def send_hi(s, p):
        at = pl.ds(p * cut, cut)
        return remote(
            walkers.at[0, at], walkers.at[2 + s, at], hi_sem, s * CHUNKS + p, on_line(s + 1, 0)
        )

    def send_far(s, p):
        at = pl.ds(p * cut, cut)
        return remote(
            walkers.at[2 + s, at], walkers.at[far + s, at], far_sem, s * CHUNKS + p, near
        )

    def send_weight(s, flip):
        slot = 1 + s + flip * steps
        return remote(weight_tile, weights.at[slot], weight_sem, slot, on_line(s + 1, flip))

    def send_far_cot(s, p):
        at = pl.ds(p * cut, cut)
        return remote(far_out.at[s, at], far_in.at[s, at], far_cot_sem, s * CHUNKS + p, near)

    def send_hi_cot(s, p):
        at = pl.ds(p * cut, cut)
        return remote(
            hi_out.at[s, at], hi_in.at[s, at], hi_cot_sem, s * CHUNKS + p, on_line(deep - 1 - s, 0)
        )

    def send_mate(u):
        return remote(mate_out.at[u], mate_in.at[u], mate_sem, u, mate)

    def send_grad(u):
        return remote(grad_out.at[u], grad_in.at[u], grad_sem, u, on_plane(*units[u]))

    load_green.wait()
    for p in range(CHUNKS):
        each(steps, lambda s: send_hi(s, p).start())
    for load in load_chol:
        load.wait()
    for p in range(CHUNKS):
        send_half(p).start()

    def start_weights(s):
        send_weight(s, 0).start()
        send_weight(s, 1).start()

    each(steps, start_weights)

    def meet(first, count, base, size):
        held = block[pl.ds(base, size), :]
        stack = walkers[pl.ds(first, count)].reshape(count * occupied, orbitals)
        swapped = lax.dot_general(held, stack, NT, preferred_element_type=F32).astype(BF16)
        pieces = [
            [
                swapped[v * occupied:(v + 1) * occupied, w * occupied:(w + 1) * occupied]
                for v in range(size // occupied)
            ]
            for w in range(count)
        ]
        wide_rows = [jnp.concatenate(line, axis=1) for line in pieces]
        cots = jnp.dot(jnp.concatenate(wide_rows, axis=0), held, preferred_element_type=F32)
        return cots.reshape(count, occupied, orbitals), pieces

    def gradients(first, scales, base, size, pieces, fresh):
        term = None
        for w, scale in enumerate(scales):
            tall = jnp.concatenate([piece.T for piece in pieces[w]], axis=0)
            more = scale * jnp.dot(tall, walkers[first + w], preferred_element_type=F32)
            term = more if term is None else term + more
        at = pl.ds(base, size)
        if fresh:
            total[at, :] = term
        else:
            total[at, :] += term

    def scale_of(slot):
        return weights[slot][0:1, 0:1]

    cots, pieces = meet(0, 1, 0, rows)
    early_cot[0] = cots[0]
    gradients(0, [weight], 0, rows, pieces, True)
    send_near.start()
    send_near_weight.start()

    for p in range(CHUNKS):
        def pass_green(s):
            send_hi(s, p).wait_recv()
            send_far(s, p).start()

        each(steps, pass_green)
        send_half(p).wait_recv()
        send_share(p).start()

    send_near.wait_recv()
    send_near_weight.wait_recv()
    each(steps, lambda s: send_weight(s, 0).wait_recv())
    group = min(far, 3)
    scales = [weight] + [scale_of(w) for w in range(group - 1)]
    cots, pieces = meet(1, group - 1, 0, rows)
    early_cot[1:group] = cots
    gradients(1, scales[1:], 0, rows, pieces, False)

    def meet_hi(s):
        cots, pieces = meet(group + s, 1, 0, rows)
        early_cot[group + s] = cots[0]
        gradients(group + s, [scale_of(group + s - 1)], 0, rows, pieces, False)

    each(far - group, meet_hi)
    for p in range(CHUNKS):
        send_share(p).wait_recv()
        base = rows + 2 * p * share
        cots, pieces = meet(0, group, base, 2 * share)
        early_cot[0:group] += cots
        if p == CHUNKS - 1:
            near_out[...] = early_cot[1].astype(BF16)
            send_near_cot.start()
        gradients(0, scales, base, 2 * share, pieces, True)

        def finish_hi(s):
            cots, pieces = meet(group + s, 1, base, 2 * share)
            early_cot[group + s] += cots[0]
            gradients(group + s, [scale_of(group + s - 1)], base, 2 * share, pieces, False)

        each(far - group, finish_hi)

    def piece_of(unit, of_core):
        flip, j = unit
        column = pl.multiple_of((((x + j) % wide) * 2 + of_core) * part, part)
        return total[pl.ds(flip * rows, rows), pl.ds(column, part)]

    def meet_far(s, last):
        for p in range(CHUNKS):
            send_far(s, p).wait_recv()
        send_weight(s, 1).wait_recv()
        cots, pieces = meet(far + s, 1, 0, 2 * rows)
        far_out[s] = cots[0].astype(BF16)
        for p in range(CHUNKS):
            send_far_cot(s, p).start()
        for flip in (1, 0):
            chosen = [pieces[0][flip * vectors:(flip + 1) * vectors]]
            gradients(far + s, [scale_of(far - 1 + s)], flip * rows, rows, chosen, False)
            if last:
                for u, unit in enumerate(units):
                    if unit[0] == flip:
                        mate_out[u] = piece_of(unit, 1 - core).astype(BF16)
                        send_mate(u).start()

    each(steps - 1, lambda s: meet_far(s, False))
    meet_far(steps - 1, True)

    for u, unit in enumerate(units[:-1]):
        send_mate(u).wait_recv()
        grad_out[u] = (piece_of(unit, core) + mate_in[u].astype(F32)).astype(BF16)
        send_grad(u).start()

    for p in range(CHUNKS):
        at = pl.ds(p * cut, cut)

        def pass_cot(s):
            send_far_cot(s, p).wait_recv()
            hi_out[s, at] = (early_cot[2 + s, at] + far_in[s, at].astype(F32)).astype(BF16)
            send_hi_cot(s, p).start()

        each(steps, pass_cot)

    last = len(units) - 1
    send_mate(last).wait_recv()
    grad = piece_of(units[last], core) + mate_in[last].astype(F32)
    send_near_cot.wait_recv()
    early_cot[0] += near_in[...].astype(F32)
    for u in range(last):
        send_grad(u).wait_recv()
        grad += grad_in[u].astype(F32)
    grad_ref[...] = grad.reshape(vectors, occupied, part)

    def add_hi(s):
        for p in range(CHUNKS):
            send_hi_cot(s, p).wait_recv()
        early_cot[0] += hi_in[s].astype(F32)

    each(steps, add_hi)
    cot_ref[0] = weight * early_cot[0]

    for copy in (send_near, send_near_weight, send_near_cot):
        copy.wait_send()
    for p in range(CHUNKS):
        send_half(p).wait_send()
        send_share(p).wait_send()

    def finish(s):
        send_weight(s, 0).wait_send()
        send_weight(s, 1).wait_send()
        for p in range(CHUNKS):
            for send in (send_hi, send_far, send_far_cot, send_hi_cot):
                send(s, p).wait_send()

    each(steps, finish)
    for u in range(len(units)):
        send_mate(u).wait_send()
    for u in range(last):
        send_grad(u).wait_send()


def hand_over(cot, grad, cot_out, grad_out):
    cot_out[...] = -cot[...]
    grad_out[...] = -grad[...]


def shards(green, chol, weight):
    deep = lax.axis_size("chol") // 4
    wide = lax.axis_size("walk") // 2
    vectors, occupied, orbitals = chol.shape
    rows = vectors * occupied
    part = orbitals // (2 * wide)
    steps = deep - 1
    units = 2 * wide
    matrix = (occupied, orbitals)
    vmem = pl.BlockSpec(memory_space=pltpu.VMEM)
    anywhere = pl.BlockSpec(memory_space=pl.ANY)
    dma = pltpu.SemaphoreType.DMA
    out_shape = (
        jax.ShapeDtypeStruct((1, occupied, orbitals), F32),
        jax.ShapeDtypeStruct((vectors, occupied, part), F32),
    )
    cot, grad = pl.pallas_call(
        functools.partial(kernel, deep, wide),
        out_shape=out_shape,
        in_specs=[pl.BlockSpec(memory_space=pltpu.SMEM), anywhere, anywhere],
        out_specs=(vmem, vmem),
        scratch_shapes=[
            pltpu.VMEM((2 * deep,) + matrix, BF16),
            pltpu.VMEM((2 * rows, orbitals), BF16),
            pltpu.VMEM((8, 128), F32),
            pltpu.VMEM((1 + 2 * steps, 8, 128), F32),
            pltpu.VMEM((2 * rows, orbitals), F32),
            pltpu.VMEM((2 + steps,) + matrix, F32),
            pltpu.VMEM(matrix, BF16),
            pltpu.VMEM(matrix, BF16),
            pltpu.VMEM((steps,) + matrix, BF16),
            pltpu.VMEM((steps,) + matrix, BF16),
            pltpu.VMEM((steps,) + matrix, BF16),
            pltpu.VMEM((steps,) + matrix, BF16),
            pltpu.VMEM((units, rows, part), BF16),
            pltpu.VMEM((units, rows, part), BF16),
            pltpu.VMEM((units - 1, rows, part), BF16),
            pltpu.VMEM((units - 1, rows, part), BF16),
            dma((1 + vectors,)), dma((2, CHUNKS)), dma((2, CHUNKS)), dma((2, 1)),
            dma((2, steps * CHUNKS)), dma((2, steps * CHUNKS)),
            dma((2, 1 + 2 * steps)), dma((2, 1)),
            dma((2, steps * CHUNKS)), dma((2, steps * CHUNKS)),
            dma((2, units)), dma((2, units - 1)),
        ],
        compiler_params=pltpu.CompilerParams(
            collective_id=0, has_side_effects=True, vmem_limit_bytes=VMEM_BYTES
        ),
    )(weight, green, chol)
    return pl.pallas_call(
        hand_over,
        out_shape=out_shape,
        in_specs=[vmem, vmem],
        out_specs=(vmem, vmem),
        compiler_params=pltpu.CompilerParams(vmem_limit_bytes=VMEM_BYTES),
    )(cot, grad)


def solution(mesh):
    in_specs = (P(("chol", "walk"), None, None), P("chol", None, None), P(("chol", "walk")))
    out_specs = (P(("chol", "walk"), None, None), P("chol", None, "walk"))
    return jax.shard_map(shards, mesh=mesh, in_specs=in_specs, out_specs=out_specs, check_vma=False)
```

```python
import functools

import jax
import jax.numpy as jnp
from jax import lax
from jax.experimental import pallas as pl
from jax.experimental.pallas import tpu as pltpu
from jax.sharding import PartitionSpec as P

MESH = pl.DeviceIdType.MESH
F32 = jnp.float32
BF16 = jnp.bfloat16
NT = (((1,), (1,)), ((), ()))
CHUNKS = 2
CUTS = 4
VMEM_BYTES = 60 * 1024 * 1024


def each(count, body):
    if count <= 8:
        for step in range(count):
            body(step)
    else:
        lax.fori_loop(0, count, lambda step, _: (body(step), 0)[1], 0)


def kernel(
    deep, wide, weight_ref, green_hbm, chol_hbm, cot_ref, grad_ref,
    walkers, block, weight_tile, weights, total, early_cot,
    near_out, near_in, far_out, far_in, hi_out, hi_in,
    mate_out, mate_in, grad_out, grad_in,
    load_sem, half_sem, share_sem, near_sem, hi_sem, far_sem, weight_sem,
    near_cot_sem, far_cot_sem, hi_cot_sem, mate_sem, grad_sem,
):
    me_c, me_k = lax.axis_index("chol"), lax.axis_index("walk")
    hi, lo, y = me_c // 4, (me_c // 2) % 2, me_c % 2
    x, core = me_k // 2, me_k % 2
    occupied, orbitals = walkers.shape[1:]
    rows = block.shape[0] // 2
    vectors = rows // occupied
    share = rows // (2 * CHUNKS)
    part = orbitals // (2 * wide)
    steps = deep - 1
    far = 2 + steps
    cut = occupied // CUTS

    def on_line(distance, flip):
        position = ((hi + distance) % deep) * 2 + (lo + flip) % 2
        return (position * 2 + y, me_k)

    def on_plane(flip, distance):
        return ((hi * 2 + lo) * 2 + (y + flip) % 2, ((x + distance) % wide) * 2 + core)

    near = on_line(0, 1)
    pair = on_plane(1, 0)
    mate = (me_c, x * 2 + (1 - core))
    units = [(flip, j) for flip in (1, 0) for j in reversed(range(wide))]

    load_green = pltpu.make_async_copy(green_hbm.at[0], walkers.at[0], load_sem.at[0])
    load_chol = [
        pltpu.make_async_copy(
            chol_hbm.at[v], block.at[pl.ds(v * occupied, occupied)], load_sem.at[1 + v]
        )
        for v in range(vectors)
    ]
    load_green.start()
    for load in load_chol:
        load.start()

    barrier = pltpu.get_barrier_semaphore()

    def greet(device):
        pl.semaphore_signal(barrier, inc=1, device_id=device, device_id_type=MESH)

    greet(near)
    greet(mate)

    def greet_line(s):
        greet(on_line(s + 1, 0))
        greet(on_line(s + 1, 1))

    each(steps, greet_line)
    for flip, j in units[:-1]:
        greet(on_plane(flip, j))
    weight = weight_ref[0]
    weight_tile[...] = jnp.full(weight_tile.shape, weight, F32)
    pl.semaphore_wait(barrier, 2 + 2 * steps + len(units) - 1)

    def remote(src, dst, sems, index, device):
        return pltpu.make_async_remote_copy(
            src_ref=src, dst_ref=dst, send_sem=sems.at[0, index], recv_sem=sems.at[1, index],
            device_id=device, device_id_type=MESH,
        )

    def send_half(p):
        start = (2 * p + core) * share
        src = pl.ds(pl.multiple_of(start, share), share)
        dst = pl.ds(pl.multiple_of(rows + start, share), share)
        return remote(block.at[src], block.at[dst], half_sem, p, pair)

    def send_share(p):
        at = pl.ds(pl.multiple_of(rows + (2 * p + core) * share, share), share)
        return remote(block.at[at], block.at[at], share_sem, p, mate)

    send_near = remote(walkers.at[0], walkers.at[1], near_sem, 0, near)
    send_near_weight = remote(weight_tile, weights.at[0], weight_sem, 0, near)
    send_near_cot = remote(near_out, near_in, near_cot_sem, 0, near)

    def send_hi(s, p):
        at = pl.ds(p * cut, cut)
        return remote(
            walkers.at[0, at], walkers.at[2 + s, at], hi_sem, s * CUTS + p, on_line(s + 1, 0)
        )

    def send_far(s, p):
        at = pl.ds(p * cut, cut)
        return remote(
            walkers.at[2 + s, at], walkers.at[far + s, at], far_sem, s * CUTS + p, near
        )

    def send_weight(s, flip):
        slot = 1 + s + flip * steps
        return remote(weight_tile, weights.at[slot], weight_sem, slot, on_line(s + 1, flip))

    def send_far_cot(s, p):
        at = pl.ds(p * cut, cut)
        return remote(far_out.at[s, at], far_in.at[s, at], far_cot_sem, s * CUTS + p, near)

    def send_hi_cot(s, p):
        at = pl.ds(p * cut, cut)
        return remote(
            hi_out.at[s, at], hi_in.at[s, at], hi_cot_sem, s * CUTS + p, on_line(deep - 1 - s, 0)
        )

    def send_mate(u):
        return remote(mate_out.at[u], mate_in.at[u], mate_sem, u, mate)

    def send_grad(u):
        return remote(grad_out.at[u], grad_in.at[u], grad_sem, u, on_plane(*units[u]))

    load_green.wait()
    for p in range(CUTS):
        each(steps, lambda s: send_hi(s, p).start())
        if p == 0:
            send_near.start()
    for load in load_chol:
        load.wait()
    for p in range(CHUNKS):
        send_half(p).start()

    def start_weights(s):
        send_weight(s, 0).start()
        send_weight(s, 1).start()

    send_near_weight.start()
    each(steps, start_weights)

    def meet(first, count, base, size):
        held = block[pl.ds(base, size), :]
        stack = walkers[pl.ds(first, count)].reshape(count * occupied, orbitals)
        swapped = lax.dot_general(held, stack, NT, preferred_element_type=F32).astype(BF16)
        pieces = [
            [
                swapped[v * occupied:(v + 1) * occupied, w * occupied:(w + 1) * occupied]
                for v in range(size // occupied)
            ]
            for w in range(count)
        ]
        wide_rows = [jnp.concatenate(line, axis=1) for line in pieces]
        cots = jnp.dot(jnp.concatenate(wide_rows, axis=0), held, preferred_element_type=F32)
        return cots.reshape(count, occupied, orbitals), pieces

    def gradients(first, scales, base, size, pieces, fresh):
        term = None
        for w, scale in enumerate(scales):
            tall = jnp.concatenate([piece.T for piece in pieces[w]], axis=0)
            more = scale * jnp.dot(tall, walkers[first + w], preferred_element_type=F32)
            term = more if term is None else term + more
        at = pl.ds(base, size)
        if fresh:
            total[at, :] = term
        else:
            total[at, :] += term

    def scale_of(slot):
        return weights[slot][0:1, 0:1]

    cots, pieces = meet(0, 1, 0, rows)
    early_cot[0] = cots[0]
    gradients(0, [weight], 0, rows, pieces, True)

    def pass_on(stage):
        for p in range(stage * CUTS // CHUNKS, (stage + 1) * CUTS // CHUNKS):
            def pass_green(s):
                send_hi(s, p).wait_recv()
                send_far(s, p).start()

            each(steps, pass_green)
        send_half(stage).wait_recv()
        send_share(stage).start()

    pass_on(0)
    send_near.wait_recv()
    send_near_weight.wait_recv()
    cots, pieces = meet(1, 1, 0, rows)
    early_cot[1] = cots[0]
    gradients(1, [scale_of(0)], 0, rows, pieces, False)
    for stage in range(1, CHUNKS):
        pass_on(stage)

    def meet_hi(s):
        send_weight(s, 0).wait_recv()
        cots, pieces = meet(2 + s, 1, 0, rows)
        early_cot[2 + s] = cots[0]
        gradients(2 + s, [scale_of(1 + s)], 0, rows, pieces, False)

    each(steps, meet_hi)
    group = min(far, 3)
    scales = [weight] + [scale_of(w) for w in range(group - 1)]
    for p in range(CHUNKS):
        send_share(p).wait_recv()
        base = rows + 2 * p * share
        cots, pieces = meet(0, group, base, 2 * share)
        early_cot[0:group] += cots
        if p == CHUNKS - 1:
            near_out[...] = early_cot[1].astype(BF16)
            send_near_cot.start()
        gradients(0, scales, base, 2 * share, pieces, True)

        def finish_hi(s):
            cots, pieces = meet(group + s, 1, base, 2 * share)
            early_cot[group + s] += cots[0]
            gradients(group + s, [scale_of(group + s - 1)], base, 2 * share, pieces, False)

        each(far - group, finish_hi)

    def piece_of(unit, of_core):
        flip, j = unit
        column = pl.multiple_of((((x + j) % wide) * 2 + of_core) * part, part)
        return total[pl.ds(flip * rows, rows), pl.ds(column, part)]

    def meet_far(s, last):
        for p in range(CUTS):
            send_far(s, p).wait_recv()
        send_weight(s, 1).wait_recv()
        cots, pieces = meet(far + s, 1, 0, 2 * rows)
        far_out[s] = cots[0].astype(BF16)
        for p in range(CUTS):
            send_far_cot(s, p).start()
        for flip in (1, 0):
            chosen = [pieces[0][flip * vectors:(flip + 1) * vectors]]
            gradients(far + s, [scale_of(far - 1 + s)], flip * rows, rows, chosen, False)
            if last:
                for u, unit in enumerate(units):
                    if unit[0] == flip:
                        mate_out[u] = piece_of(unit, 1 - core).astype(BF16)
                        send_mate(u).start()

    each(steps - 1, lambda s: meet_far(s, False))
    meet_far(steps - 1, True)

    def pass_cots(p):
        at = pl.ds(p * cut, cut)

        def pass_cot(s):
            send_far_cot(s, p).wait_recv()
            hi_out[s, at] = (early_cot[2 + s, at] + far_in[s, at].astype(F32)).astype(BF16)
            send_hi_cot(s, p).start()

        each(steps, pass_cot)

    for u, unit in enumerate(units[:-1]):
        send_mate(u).wait_recv()
        grad_out[u] = (piece_of(unit, core) + mate_in[u].astype(F32)).astype(BF16)
        send_grad(u).start()
        if u < CUTS:
            pass_cots(u)
    for p in range(min(CUTS, len(units) - 1), CUTS):
        pass_cots(p)

    last = len(units) - 1
    send_mate(last).wait_recv()
    grad = piece_of(units[last], core) + mate_in[last].astype(F32)
    send_near_cot.wait_recv()
    early_cot[0] += near_in[...].astype(F32)
    for u in range(last):
        send_grad(u).wait_recv()
        grad += grad_in[u].astype(F32)
    grad_ref[...] = grad.reshape(vectors, occupied, part)

    def add_hi(s):
        for p in range(CUTS):
            send_hi_cot(s, p).wait_recv()
        early_cot[0] += hi_in[s].astype(F32)

    each(steps, add_hi)
    cot_ref[0] = weight * early_cot[0]

    for copy in (send_near, send_near_weight, send_near_cot):
        copy.wait_send()
    for p in range(CHUNKS):
        send_half(p).wait_send()
        send_share(p).wait_send()

    def finish(s):
        send_weight(s, 0).wait_send()
        send_weight(s, 1).wait_send()
        for p in range(CUTS):
            for send in (send_hi, send_far, send_far_cot, send_hi_cot):
                send(s, p).wait_send()

    each(steps, finish)
    for u in range(len(units)):
        send_mate(u).wait_send()
    for u in range(last):
        send_grad(u).wait_send()


def hand_over(cot, grad, cot_out, grad_out):
    cot_out[...] = -cot[...]
    grad_out[...] = -grad[...]


def shards(green, chol, weight):
    deep = lax.axis_size("chol") // 4
    wide = lax.axis_size("walk") // 2
    vectors, occupied, orbitals = chol.shape
    rows = vectors * occupied
    part = orbitals // (2 * wide)
    steps = deep - 1
    units = 2 * wide
    matrix = (occupied, orbitals)
    vmem = pl.BlockSpec(memory_space=pltpu.VMEM)
    anywhere = pl.BlockSpec(memory_space=pl.ANY)
    dma = pltpu.SemaphoreType.DMA
    out_shape = (
        jax.ShapeDtypeStruct((1, occupied, orbitals), F32),
        jax.ShapeDtypeStruct((vectors, occupied, part), F32),
    )
    cot, grad = pl.pallas_call(
        functools.partial(kernel, deep, wide),
        out_shape=out_shape,
        in_specs=[pl.BlockSpec(memory_space=pltpu.SMEM), anywhere, anywhere],
        out_specs=(vmem, vmem),
        scratch_shapes=[
            pltpu.VMEM((2 * deep,) + matrix, BF16),
            pltpu.VMEM((2 * rows, orbitals), BF16),
            pltpu.VMEM((8, 128), F32),
            pltpu.VMEM((1 + 2 * steps, 8, 128), F32),
            pltpu.VMEM((2 * rows, orbitals), F32),
            pltpu.VMEM((2 + steps,) + matrix, F32),
            pltpu.VMEM(matrix, BF16),
            pltpu.VMEM(matrix, BF16),
            pltpu.VMEM((steps,) + matrix, BF16),
            pltpu.VMEM((steps,) + matrix, BF16),
            pltpu.VMEM((steps,) + matrix, BF16),
            pltpu.VMEM((steps,) + matrix, BF16),
            pltpu.VMEM((units, rows, part), BF16),
            pltpu.VMEM((units, rows, part), BF16),
            pltpu.VMEM((units - 1, rows, part), BF16),
            pltpu.VMEM((units - 1, rows, part), BF16),
            dma((1 + vectors,)), dma((2, CHUNKS)), dma((2, CHUNKS)), dma((2, 1)),
            dma((2, steps * CUTS)), dma((2, steps * CUTS)),
            dma((2, 1 + 2 * steps)), dma((2, 1)),
            dma((2, steps * CUTS)), dma((2, steps * CUTS)),
            dma((2, units)), dma((2, units - 1)),
        ],
        compiler_params=pltpu.CompilerParams(
            collective_id=0, has_side_effects=True, vmem_limit_bytes=VMEM_BYTES
        ),
    )(weight, green, chol)
    return pl.pallas_call(
        hand_over,
        out_shape=out_shape,
        in_specs=[vmem, vmem],
        out_specs=(vmem, vmem),
        compiler_params=pltpu.CompilerParams(vmem_limit_bytes=VMEM_BYTES),
    )(cot, grad)


def solution(mesh):
    in_specs = (P(("chol", "walk"), None, None), P("chol", None, None), P(("chol", "walk")))
    out_specs = (P(("chol", "walk"), None, None), P("chol", None, "walk"))
    return jax.shard_map(shards, mesh=mesh, in_specs=in_specs, out_specs=out_specs, check_vma=False)
```

```python
import functools

import jax
import jax.numpy as jnp
from jax import lax
from jax.experimental import pallas as pl
from jax.experimental.pallas import tpu as pltpu
from jax.sharding import PartitionSpec as P

MESH = pl.DeviceIdType.MESH
F32 = jnp.float32
BF16 = jnp.bfloat16
NT = (((1,), (1,)), ((), ()))
CHUNKS = 2
SUMMED = 1
VMEM_BYTES = 60 * 1024 * 1024


def each(count, body):
    if count <= 8:
        for step in range(count):
            body(step)
    else:
        lax.fori_loop(0, count, lambda step, _: (body(step), 0)[1], 0)


def kernel(
    deep, wide, weight_ref, green_hbm, chol_hbm, cot_ref, grad_ref,
    walkers, block, weight_tile, weights, total, early_cot,
    near_out, near_in, far_out, far_in, hi_out, hi_in,
    mate_out, mate_in, grad_out, grad_in,
    load_sem, half_sem, share_sem, near_sem, hi_sem, far_sem, weight_sem,
    near_cot_sem, far_cot_sem, hi_cot_sem, mate_sem, grad_sem,
):
    me_c, me_k = lax.axis_index("chol"), lax.axis_index("walk")
    hi, lo, y = me_c // 4, (me_c // 2) % 2, me_c % 2
    x, core = me_k // 2, me_k % 2
    occupied, orbitals = walkers.shape[1:]
    rows = block.shape[0] // 2
    vectors = rows // occupied
    share = rows // (2 * CHUNKS)
    part = orbitals // (2 * wide)
    steps = deep - 1
    far = 2 + steps
    cut = occupied // CHUNKS

    def on_line(distance, flip):
        position = ((hi + distance) % deep) * 2 + (lo + flip) % 2
        return (position * 2 + y, me_k)

    def on_plane(flip, distance):
        return ((hi * 2 + lo) * 2 + (y + flip) % 2, ((x + distance) % wide) * 2 + core)

    near = on_line(0, 1)
    pair = on_plane(1, 0)
    mate = (me_c, x * 2 + (1 - core))
    units = [(flip, j) for flip in (1, 0) for j in reversed(range(wide))]

    load_green = pltpu.make_async_copy(green_hbm.at[0], walkers.at[0], load_sem.at[0])
    load_chol = [
        pltpu.make_async_copy(
            chol_hbm.at[v], block.at[pl.ds(v * occupied, occupied)], load_sem.at[1 + v]
        )
        for v in range(vectors)
    ]
    load_green.start()
    for load in load_chol:
        load.start()

    barrier = pltpu.get_barrier_semaphore()

    def greet(device):
        pl.semaphore_signal(barrier, inc=1, device_id=device, device_id_type=MESH)

    greet(near)
    greet(mate)

    def greet_line(s):
        greet(on_line(s + 1, 0))
        greet(on_line(s + 1, 1))

    each(steps, greet_line)
    for flip, j in units[:-1]:
        greet(on_plane(flip, j))
    weight = weight_ref[0]
    weight_tile[...] = jnp.full(weight_tile.shape, weight, F32)
    pl.semaphore_wait(barrier, 2 + 2 * steps + len(units) - 1)

    def remote(src, dst, sems, index, device):
        return pltpu.make_async_remote_copy(
            src_ref=src, dst_ref=dst, send_sem=sems.at[0, index], recv_sem=sems.at[1, index],
            device_id=device, device_id_type=MESH,
        )

    def send_half(p):
        start = (2 * p + core) * share
        src = pl.ds(pl.multiple_of(start, share), share)
        dst = pl.ds(pl.multiple_of(rows + start, share), share)
        return remote(block.at[src], block.at[dst], half_sem, p, pair)

    def send_share(p):
        at = pl.ds(pl.multiple_of(rows + (2 * p + core) * share, share), share)
        return remote(block.at[at], block.at[at], share_sem, p, mate)

    send_near = remote(walkers.at[0], walkers.at[1], near_sem, 0, near)
    send_near_weight = remote(weight_tile, weights.at[0], weight_sem, 0, near)
    send_near_cot = remote(near_out, near_in, near_cot_sem, 0, near)

    def send_hi(s, p):
        at = pl.ds(p * cut, cut)
        return remote(
            walkers.at[0, at], walkers.at[2 + s, at], hi_sem, s * CHUNKS + p, on_line(s + 1, 0)
        )

    def send_far(s, p):
        at = pl.ds(p * cut, cut)
        return remote(
            walkers.at[2 + s, at], walkers.at[far + s, at], far_sem, s * CHUNKS + p, near
        )

    def send_weight(s, flip):
        slot = 1 + s + flip * steps
        return remote(weight_tile, weights.at[slot], weight_sem, slot, on_line(s + 1, flip))

    def send_far_cot(s, p):
        at = pl.ds(p * cut, cut)
        owner = near if p < SUMMED else on_line(deep - 1 - s, 1)
        return remote(far_out.at[s, at], far_in.at[s, at], far_cot_sem, s * CHUNKS + p, owner)

    def send_hi_cot(s, p):
        at = pl.ds(p * cut, cut)
        return remote(
            hi_out.at[s, at], hi_in.at[s, at], hi_cot_sem, s * CHUNKS + p, on_line(deep - 1 - s, 0)
        )

    def send_mate(u):
        return remote(mate_out.at[u], mate_in.at[u], mate_sem, u, mate)

    def send_grad(u):
        return remote(grad_out.at[u], grad_in.at[u], grad_sem, u, on_plane(*units[u]))

    load_green.wait()
    for p in range(CHUNKS):
        each(steps, lambda s: send_hi(s, p).start())
    for load in load_chol:
        load.wait()
    for p in range(CHUNKS):
        send_half(p).start()

    def start_weights(s):
        send_weight(s, 0).start()
        send_weight(s, 1).start()

    each(steps, start_weights)

    def meet(first, count, base, size):
        held = block[pl.ds(base, size), :]
        stack = walkers[pl.ds(first, count)].reshape(count * occupied, orbitals)
        swapped = lax.dot_general(held, stack, NT, preferred_element_type=F32).astype(BF16)
        pieces = [
            [
                swapped[v * occupied:(v + 1) * occupied, w * occupied:(w + 1) * occupied]
                for v in range(size // occupied)
            ]
            for w in range(count)
        ]
        wide_rows = [jnp.concatenate(line, axis=1) for line in pieces]
        cots = jnp.dot(jnp.concatenate(wide_rows, axis=0), held, preferred_element_type=F32)
        return cots.reshape(count, occupied, orbitals), pieces

    def gradients(first, scales, base, size, pieces, fresh):
        term = None
        for w, scale in enumerate(scales):
            tall = jnp.concatenate([piece.T for piece in pieces[w]], axis=0)
            more = scale * jnp.dot(tall, walkers[first + w], preferred_element_type=F32)
            term = more if term is None else term + more
        at = pl.ds(base, size)
        if fresh:
            total[at, :] = term
        else:
            total[at, :] += term

    def scale_of(slot):
        return weights[slot][0:1, 0:1]

    cots, pieces = meet(0, 1, 0, rows)
    early_cot[0] = cots[0]
    gradients(0, [weight], 0, rows, pieces, True)
    send_near.start()
    send_near_weight.start()

    for p in range(CHUNKS):
        def pass_green(s):
            send_hi(s, p).wait_recv()
            send_far(s, p).start()

        each(steps, pass_green)
        send_half(p).wait_recv()
        send_share(p).start()

    send_near.wait_recv()
    send_near_weight.wait_recv()
    each(steps, lambda s: send_weight(s, 0).wait_recv())
    group = min(far, 3)
    scales = [weight] + [scale_of(w) for w in range(group - 1)]
    cots, pieces = meet(1, group - 1, 0, rows)
    early_cot[1:group] = cots
    gradients(1, scales[1:], 0, rows, pieces, False)

    def meet_hi(s):
        cots, pieces = meet(group + s, 1, 0, rows)
        early_cot[group + s] = cots[0]
        gradients(group + s, [scale_of(group + s - 1)], 0, rows, pieces, False)

    each(far - group, meet_hi)
    for p in range(CHUNKS):
        send_share(p).wait_recv()
        base = rows + 2 * p * share
        cots, pieces = meet(0, group, base, 2 * share)
        early_cot[0:group] += cots
        if p == CHUNKS - 1:
            near_out[...] = early_cot[1].astype(BF16)
            send_near_cot.start()

            def send_home(s):
                for p in range(SUMMED, CHUNKS):
                    at = pl.ds(p * cut, cut)
                    hi_out[s, at] = early_cot[2 + s, at].astype(BF16)
                    send_hi_cot(s, p).start()

            each(group - 2, send_home)
        gradients(0, scales, base, 2 * share, pieces, True)

        def finish_hi(s):
            cots, pieces = meet(group + s, 1, base, 2 * share)
            early_cot[group + s] += cots[0]
            if p == CHUNKS - 1:
                send_home(group - 2 + s)
            gradients(group + s, [scale_of(group + s - 1)], base, 2 * share, pieces, False)

        each(far - group, finish_hi)

    def piece_of(unit, of_core):
        flip, j = unit
        column = pl.multiple_of((((x + j) % wide) * 2 + of_core) * part, part)
        return total[pl.ds(flip * rows, rows), pl.ds(column, part)]

    def meet_far(s, last):
        for p in range(CHUNKS):
            send_far(s, p).wait_recv()
        send_weight(s, 1).wait_recv()
        cots, pieces = meet(far + s, 1, 0, 2 * rows)
        far_out[s] = cots[0].astype(BF16)
        for p in range(CHUNKS):
            send_far_cot(s, p).start()
        for flip in (1, 0):
            chosen = [pieces[0][flip * vectors:(flip + 1) * vectors]]
            gradients(far + s, [scale_of(far - 1 + s)], flip * rows, rows, chosen, False)
            if last:
                for u, unit in enumerate(units):
                    if unit[0] == flip:
                        mate_out[u] = piece_of(unit, 1 - core).astype(BF16)
                        send_mate(u).start()

    each(steps - 1, lambda s: meet_far(s, False))
    meet_far(steps - 1, True)

    def pass_cots(p):
        at = pl.ds(p * cut, cut)

        def pass_cot(s):
            send_far_cot(s, p).wait_recv()
            hi_out[s, at] = (early_cot[2 + s, at] + far_in[s, at].astype(F32)).astype(BF16)
            send_hi_cot(s, p).start()

        each(steps, pass_cot)

    for u, unit in enumerate(units[:-1]):
        send_mate(u).wait_recv()
        grad_out[u] = (piece_of(unit, core) + mate_in[u].astype(F32)).astype(BF16)
        send_grad(u).start()
        if u == 0:
            for p in range(SUMMED):
                pass_cots(p)

    last = len(units) - 1
    send_mate(last).wait_recv()
    grad = piece_of(units[last], core) + mate_in[last].astype(F32)
    send_near_cot.wait_recv()
    early_cot[0] += near_in[...].astype(F32)
    for u in range(last):
        send_grad(u).wait_recv()
        grad += grad_in[u].astype(F32)
    grad_ref[...] = grad.reshape(vectors, occupied, part)

    def add_hi(s):
        for p in range(CHUNKS):
            send_hi_cot(s, p).wait_recv()
        early_cot[0] += hi_in[s].astype(F32)
        for p in range(SUMMED, CHUNKS):
            at = pl.ds(p * cut, cut)
            send_far_cot(s, p).wait_recv()
            early_cot[0, at] += far_in[s, at].astype(F32)

    each(steps, add_hi)
    cot_ref[0] = weight * early_cot[0]

    for copy in (send_near, send_near_weight, send_near_cot):
        copy.wait_send()
    for p in range(CHUNKS):
        send_half(p).wait_send()
        send_share(p).wait_send()

    def finish(s):
        send_weight(s, 0).wait_send()
        send_weight(s, 1).wait_send()
        for p in range(CHUNKS):
            for send in (send_hi, send_far, send_far_cot, send_hi_cot):
                send(s, p).wait_send()

    each(steps, finish)
    for u in range(len(units)):
        send_mate(u).wait_send()
    for u in range(last):
        send_grad(u).wait_send()


def hand_over(cot, grad, cot_out, grad_out):
    cot_out[...] = -cot[...]
    grad_out[...] = -grad[...]


def shards(green, chol, weight):
    deep = lax.axis_size("chol") // 4
    wide = lax.axis_size("walk") // 2
    vectors, occupied, orbitals = chol.shape
    rows = vectors * occupied
    part = orbitals // (2 * wide)
    steps = deep - 1
    units = 2 * wide
    matrix = (occupied, orbitals)
    vmem = pl.BlockSpec(memory_space=pltpu.VMEM)
    anywhere = pl.BlockSpec(memory_space=pl.ANY)
    dma = pltpu.SemaphoreType.DMA
    out_shape = (
        jax.ShapeDtypeStruct((1, occupied, orbitals), F32),
        jax.ShapeDtypeStruct((vectors, occupied, part), F32),
    )
    cot, grad = pl.pallas_call(
        functools.partial(kernel, deep, wide),
        out_shape=out_shape,
        in_specs=[pl.BlockSpec(memory_space=pltpu.SMEM), anywhere, anywhere],
        out_specs=(vmem, vmem),
        scratch_shapes=[
            pltpu.VMEM((2 * deep,) + matrix, BF16),
            pltpu.VMEM((2 * rows, orbitals), BF16),
            pltpu.VMEM((8, 128), F32),
            pltpu.VMEM((1 + 2 * steps, 8, 128), F32),
            pltpu.VMEM((2 * rows, orbitals), F32),
            pltpu.VMEM((2 + steps,) + matrix, F32),
            pltpu.VMEM(matrix, BF16),
            pltpu.VMEM(matrix, BF16),
            pltpu.VMEM((steps,) + matrix, BF16),
            pltpu.VMEM((steps,) + matrix, BF16),
            pltpu.VMEM((steps,) + matrix, BF16),
            pltpu.VMEM((steps,) + matrix, BF16),
            pltpu.VMEM((units, rows, part), BF16),
            pltpu.VMEM((units, rows, part), BF16),
            pltpu.VMEM((units - 1, rows, part), BF16),
            pltpu.VMEM((units - 1, rows, part), BF16),
            dma((1 + vectors,)), dma((2, CHUNKS)), dma((2, CHUNKS)), dma((2, 1)),
            dma((2, steps * CHUNKS)), dma((2, steps * CHUNKS)),
            dma((2, 1 + 2 * steps)), dma((2, 1)),
            dma((2, steps * CHUNKS)), dma((2, steps * CHUNKS)),
            dma((2, units)), dma((2, units - 1)),
        ],
        compiler_params=pltpu.CompilerParams(
            collective_id=0, has_side_effects=True, vmem_limit_bytes=VMEM_BYTES
        ),
    )(weight, green, chol)
    return pl.pallas_call(
        hand_over,
        out_shape=out_shape,
        in_specs=[vmem, vmem],
        out_specs=(vmem, vmem),
        compiler_params=pltpu.CompilerParams(vmem_limit_bytes=VMEM_BYTES),
    )(cot, grad)


def solution(mesh):
    in_specs = (P(("chol", "walk"), None, None), P("chol", None, None), P(("chol", "walk")))
    out_specs = (P(("chol", "walk"), None, None), P("chol", None, "walk"))
    return jax.shard_map(shards, mesh=mesh, in_specs=in_specs, out_specs=out_specs, check_vma=False)
```

```python
import functools

import jax
import jax.numpy as jnp
from jax import lax
from jax.experimental import pallas as pl
from jax.experimental.pallas import tpu as pltpu
from jax.sharding import PartitionSpec as P

MESH = pl.DeviceIdType.MESH
F32 = jnp.float32
BF16 = jnp.bfloat16
NT = (((1,), (1,)), ((), ()))
CHUNKS = 2
SUMMED = 1
VMEM_BYTES = 60 * 1024 * 1024


def each(count, body):
    if count <= 8:
        for step in range(count):
            body(step)
    else:
        lax.fori_loop(0, count, lambda step, _: (body(step), 0)[1], 0)


def kernel(
    deep, wide, weight_ref, green_hbm, chol_hbm, cot_ref, grad_ref,
    walkers, block, weight_tile, weights, total, early_cot,
    near_out, near_in, far_out, far_in, hi_out, hi_in,
    mate_out, mate_in, grad_out, grad_in,
    load_sem, half_sem, share_sem, near_sem, hi_sem, far_sem, weight_sem,
    near_cot_sem, far_cot_sem, hi_cot_sem, mate_sem, grad_sem,
):
    me_c, me_k = lax.axis_index("chol"), lax.axis_index("walk")
    hi, lo, y = me_c // 4, (me_c // 2) % 2, me_c % 2
    x, core = me_k // 2, me_k % 2
    occupied, orbitals = walkers.shape[1:]
    rows = block.shape[0] // 2
    vectors = rows // occupied
    share = rows // (2 * CHUNKS)
    part = orbitals // (2 * wide)
    steps = deep - 1
    far = 2 + steps
    cut = occupied // CHUNKS

    def on_line(distance, flip):
        position = ((hi + distance) % deep) * 2 + (lo + flip) % 2
        return (position * 2 + y, me_k)

    def on_plane(flip, distance):
        return ((hi * 2 + lo) * 2 + (y + flip) % 2, ((x + distance) % wide) * 2 + core)

    near = on_line(0, 1)
    pair = on_plane(1, 0)
    mate = (me_c, x * 2 + (1 - core))
    units = [(flip, j) for flip in (1, 0) for j in reversed(range(wide))]

    load_green = pltpu.make_async_copy(green_hbm.at[0], walkers.at[0], load_sem.at[0])
    load_chol = [
        pltpu.make_async_copy(
            chol_hbm.at[v], block.at[pl.ds(v * occupied, occupied)], load_sem.at[1 + v]
        )
        for v in range(vectors)
    ]
    load_green.start()
    for load in load_chol:
        load.start()

    barrier = pltpu.get_barrier_semaphore()

    def greet(device):
        pl.semaphore_signal(barrier, inc=1, device_id=device, device_id_type=MESH)

    greet(near)
    greet(mate)

    def greet_line(s):
        greet(on_line(s + 1, 0))
        greet(on_line(s + 1, 1))

    each(steps, greet_line)
    for flip, j in units[:-1]:
        greet(on_plane(flip, j))
    weight = weight_ref[0]
    weight_tile[...] = jnp.full(weight_tile.shape, weight, F32)
    pl.semaphore_wait(barrier, 2 + 2 * steps + len(units) - 1)

    def remote(src, dst, sems, index, device):
        return pltpu.make_async_remote_copy(
            src_ref=src, dst_ref=dst, send_sem=sems.at[0, index], recv_sem=sems.at[1, index],
            device_id=device, device_id_type=MESH,
        )

    def send_half(p):
        start = (2 * p + core) * share
        src = pl.ds(pl.multiple_of(start, share), share)
        dst = pl.ds(pl.multiple_of(rows + start, share), share)
        return remote(block.at[src], block.at[dst], half_sem, p, pair)

    def send_share(p):
        at = pl.ds(pl.multiple_of(rows + (2 * p + core) * share, share), share)
        return remote(block.at[at], block.at[at], share_sem, p, mate)

    send_near = remote(walkers.at[0], walkers.at[1], near_sem, 0, near)
    send_near_weight = remote(weight_tile, weights.at[0], weight_sem, 0, near)
    send_near_cot = remote(near_out, near_in, near_cot_sem, 0, near)

    def send_hi(s, p):
        at = pl.ds(p * cut, cut)
        return remote(
            walkers.at[0, at], walkers.at[2 + s, at], hi_sem, s * CHUNKS + p, on_line(s + 1, 0)
        )

    def send_far(s, p):
        at = pl.ds(p * cut, cut)
        return remote(
            walkers.at[2 + s, at], walkers.at[far + s, at], far_sem, s * CHUNKS + p, near
        )

    def send_weight(s, flip):
        slot = 1 + s + flip * steps
        return remote(weight_tile, weights.at[slot], weight_sem, slot, on_line(s + 1, flip))

    def send_far_cot(s, p):
        at = pl.ds(p * cut, cut)
        owner = near if p < SUMMED else on_line(deep - 1 - s, 1)
        return remote(far_out.at[s, at], far_in.at[s, at], far_cot_sem, s * CHUNKS + p, owner)

    def send_hi_cot(s, p):
        at = pl.ds(p * cut, cut)
        return remote(
            hi_out.at[s, at], hi_in.at[s, at], hi_cot_sem, s * CHUNKS + p, on_line(deep - 1 - s, 0)
        )

    def send_mate(u):
        return remote(mate_out.at[u], mate_in.at[u], mate_sem, u, mate)

    def send_grad(u):
        return remote(grad_out.at[u], grad_in.at[u], grad_sem, u, on_plane(*units[u]))

    load_green.wait()
    for p in range(CHUNKS):
        each(steps, lambda s: send_hi(s, p).start())
    send_near.start()
    for load in load_chol:
        load.wait()
    for p in range(CHUNKS):
        send_half(p).start()

    def start_weights(s):
        send_weight(s, 0).start()
        send_weight(s, 1).start()

    send_near_weight.start()
    each(steps, start_weights)

    def meet(first, count, base, size):
        held = block[pl.ds(base, size), :]
        stack = walkers[pl.ds(first, count)].reshape(count * occupied, orbitals)
        swapped = lax.dot_general(held, stack, NT, preferred_element_type=F32).astype(BF16)
        pieces = [
            [
                swapped[v * occupied:(v + 1) * occupied, w * occupied:(w + 1) * occupied]
                for v in range(size // occupied)
            ]
            for w in range(count)
        ]
        wide_rows = [jnp.concatenate(line, axis=1) for line in pieces]
        cots = jnp.dot(jnp.concatenate(wide_rows, axis=0), held, preferred_element_type=F32)
        return cots.reshape(count, occupied, orbitals), pieces

    def gradients(first, scales, base, size, pieces, fresh):
        term = None
        for w, scale in enumerate(scales):
            tall = jnp.concatenate([piece.T for piece in pieces[w]], axis=0)
            more = scale * jnp.dot(tall, walkers[first + w], preferred_element_type=F32)
            term = more if term is None else term + more
        at = pl.ds(base, size)
        if fresh:
            total[at, :] = term
        else:
            total[at, :] += term

    def scale_of(slot):
        return weights[slot][0:1, 0:1]

    cots, pieces = meet(0, 1, 0, rows)
    early_cot[0] = cots[0]
    gradients(0, [weight], 0, rows, pieces, True)

    def pass_on(p):
        def pass_green(s):
            send_hi(s, p).wait_recv()
            send_far(s, p).start()

        each(steps, pass_green)
        send_half(p).wait_recv()
        send_share(p).start()

    pass_on(0)
    send_near.wait_recv()
    send_near_weight.wait_recv()
    cots, pieces = meet(1, 1, 0, rows)
    early_cot[1] = cots[0]
    gradients(1, [scale_of(0)], 0, rows, pieces, False)
    for p in range(1, CHUNKS):
        pass_on(p)

    def meet_hi(s):
        send_weight(s, 0).wait_recv()
        cots, pieces = meet(2 + s, 1, 0, rows)
        early_cot[2 + s] = cots[0]
        gradients(2 + s, [scale_of(1 + s)], 0, rows, pieces, False)

    each(steps, meet_hi)
    group = min(far, 3)
    scales = [weight] + [scale_of(w) for w in range(group - 1)]
    for p in range(CHUNKS):
        send_share(p).wait_recv()
        base = rows + 2 * p * share
        cots, pieces = meet(0, group, base, 2 * share)
        early_cot[0:group] += cots
        if p == CHUNKS - 1:
            near_out[...] = early_cot[1].astype(BF16)
            send_near_cot.start()

            def send_home(s):
                for p in range(SUMMED, CHUNKS):
                    at = pl.ds(p * cut, cut)
                    hi_out[s, at] = early_cot[2 + s, at].astype(BF16)
                    send_hi_cot(s, p).start()

            each(group - 2, send_home)
        gradients(0, scales, base, 2 * share, pieces, True)

        def finish_hi(s):
            cots, pieces = meet(group + s, 1, base, 2 * share)
            early_cot[group + s] += cots[0]
            if p == CHUNKS - 1:
                send_home(group - 2 + s)
            gradients(group + s, [scale_of(group + s - 1)], base, 2 * share, pieces, False)

        each(far - group, finish_hi)

    def piece_of(unit, of_core):
        flip, j = unit
        column = pl.multiple_of((((x + j) % wide) * 2 + of_core) * part, part)
        return total[pl.ds(flip * rows, rows), pl.ds(column, part)]

    def meet_far(s, last):
        for p in range(CHUNKS):
            send_far(s, p).wait_recv()
        send_weight(s, 1).wait_recv()
        cots, pieces = meet(far + s, 1, 0, 2 * rows)
        far_out[s] = cots[0].astype(BF16)
        for p in range(CHUNKS):
            send_far_cot(s, p).start()
        for flip in (1, 0):
            chosen = [pieces[0][flip * vectors:(flip + 1) * vectors]]
            gradients(far + s, [scale_of(far - 1 + s)], flip * rows, rows, chosen, False)
            if last:
                for u, unit in enumerate(units):
                    if unit[0] == flip:
                        mate_out[u] = piece_of(unit, 1 - core).astype(BF16)
                        send_mate(u).start()

    each(steps - 1, lambda s: meet_far(s, False))
    meet_far(steps - 1, True)

    def pass_cots(p):
        at = pl.ds(p * cut, cut)

        def pass_cot(s):
            send_far_cot(s, p).wait_recv()
            hi_out[s, at] = (early_cot[2 + s, at] + far_in[s, at].astype(F32)).astype(BF16)
            send_hi_cot(s, p).start()

        each(steps, pass_cot)

    for u, unit in enumerate(units[:-1]):
        send_mate(u).wait_recv()
        grad_out[u] = (piece_of(unit, core) + mate_in[u].astype(F32)).astype(BF16)
        send_grad(u).start()
        if u == 0:
            for p in range(SUMMED):
                pass_cots(p)

    last = len(units) - 1
    send_mate(last).wait_recv()
    grad = piece_of(units[last], core) + mate_in[last].astype(F32)
    send_near_cot.wait_recv()
    early_cot[0] += near_in[...].astype(F32)
    for u in range(last):
        send_grad(u).wait_recv()
        grad += grad_in[u].astype(F32)
    grad_ref[...] = grad.reshape(vectors, occupied, part)

    def add_hi(s):
        for p in range(CHUNKS):
            send_hi_cot(s, p).wait_recv()
        early_cot[0] += hi_in[s].astype(F32)
        for p in range(SUMMED, CHUNKS):
            at = pl.ds(p * cut, cut)
            send_far_cot(s, p).wait_recv()
            early_cot[0, at] += far_in[s, at].astype(F32)

    each(steps, add_hi)
    cot_ref[0] = weight * early_cot[0]

    for copy in (send_near, send_near_weight, send_near_cot):
        copy.wait_send()
    for p in range(CHUNKS):
        send_half(p).wait_send()
        send_share(p).wait_send()

    def finish(s):
        send_weight(s, 0).wait_send()
        send_weight(s, 1).wait_send()
        for p in range(CHUNKS):
            for send in (send_hi, send_far, send_far_cot, send_hi_cot):
                send(s, p).wait_send()

    each(steps, finish)
    for u in range(len(units)):
        send_mate(u).wait_send()
    for u in range(last):
        send_grad(u).wait_send()


def hand_over(cot, grad, cot_out, grad_out):
    cot_out[...] = -cot[...]
    grad_out[...] = -grad[...]


def shards(green, chol, weight):
    deep = lax.axis_size("chol") // 4
    wide = lax.axis_size("walk") // 2
    vectors, occupied, orbitals = chol.shape
    rows = vectors * occupied
    part = orbitals // (2 * wide)
    steps = deep - 1
    units = 2 * wide
    matrix = (occupied, orbitals)
    vmem = pl.BlockSpec(memory_space=pltpu.VMEM)
    anywhere = pl.BlockSpec(memory_space=pl.ANY)
    dma = pltpu.SemaphoreType.DMA
    out_shape = (
        jax.ShapeDtypeStruct((1, occupied, orbitals), F32),
        jax.ShapeDtypeStruct((vectors, occupied, part), F32),
    )
    cot, grad = pl.pallas_call(
        functools.partial(kernel, deep, wide),
        out_shape=out_shape,
        in_specs=[pl.BlockSpec(memory_space=pltpu.SMEM), anywhere, anywhere],
        out_specs=(vmem, vmem),
        scratch_shapes=[
            pltpu.VMEM((2 * deep,) + matrix, BF16),
            pltpu.VMEM((2 * rows, orbitals), BF16),
            pltpu.VMEM((8, 128), F32),
            pltpu.VMEM((1 + 2 * steps, 8, 128), F32),
            pltpu.VMEM((2 * rows, orbitals), F32),
            pltpu.VMEM((2 + steps,) + matrix, F32),
            pltpu.VMEM(matrix, BF16),
            pltpu.VMEM(matrix, BF16),
            pltpu.VMEM((steps,) + matrix, BF16),
            pltpu.VMEM((steps,) + matrix, BF16),
            pltpu.VMEM((steps,) + matrix, BF16),
            pltpu.VMEM((steps,) + matrix, BF16),
            pltpu.VMEM((units, rows, part), BF16),
            pltpu.VMEM((units, rows, part), BF16),
            pltpu.VMEM((units - 1, rows, part), BF16),
            pltpu.VMEM((units - 1, rows, part), BF16),
            dma((1 + vectors,)), dma((2, CHUNKS)), dma((2, CHUNKS)), dma((2, 1)),
            dma((2, steps * CHUNKS)), dma((2, steps * CHUNKS)),
            dma((2, 1 + 2 * steps)), dma((2, 1)),
            dma((2, steps * CHUNKS)), dma((2, steps * CHUNKS)),
            dma((2, units)), dma((2, units - 1)),
        ],
        compiler_params=pltpu.CompilerParams(
            collective_id=0, has_side_effects=True, vmem_limit_bytes=VMEM_BYTES
        ),
    )(weight, green, chol)
    return pl.pallas_call(
        hand_over,
        out_shape=out_shape,
        in_specs=[vmem, vmem],
        out_specs=(vmem, vmem),
        compiler_params=pltpu.CompilerParams(vmem_limit_bytes=VMEM_BYTES),
    )(cot, grad)


def solution(mesh):
    in_specs = (P(("chol", "walk"), None, None), P("chol", None, None), P(("chol", "walk")))
    out_specs = (P(("chol", "walk"), None, None), P("chol", None, "walk"))
    return jax.shard_map(shards, mesh=mesh, in_specs=in_specs, out_specs=out_specs, check_vma=False)
```

```python
import functools

import jax
import jax.numpy as jnp
from jax import lax
from jax.experimental import pallas as pl
from jax.experimental.pallas import tpu as pltpu
from jax.sharding import PartitionSpec as P

MESH = pl.DeviceIdType.MESH
F32 = jnp.float32
BF16 = jnp.bfloat16
NT = (((1,), (1,)), ((), ()))
CHUNKS = 2
SUMMED = 1
VMEM_BYTES = 60 * 1024 * 1024


def each(count, body):
    if count <= 8:
        for step in range(count):
            body(step)
    else:
        lax.fori_loop(0, count, lambda step, _: (body(step), 0)[1], 0)


def kernel(
    deep, wide, weight_ref, green_hbm, chol_hbm, cot_ref, grad_ref,
    walkers, block, weight_tile, weights, total, early_cot,
    near_out, near_in, far_out, far_in, hi_out, hi_in,
    mate_out, mate_in, grad_out, grad_in,
    load_sem, half_sem, share_sem, near_sem, hi_sem, far_sem, weight_sem,
    near_cot_sem, far_cot_sem, hi_cot_sem, mate_sem, grad_sem,
):
    me_c, me_k = lax.axis_index("chol"), lax.axis_index("walk")
    hi, lo, y = me_c // 4, (me_c // 2) % 2, me_c % 2
    x, core = me_k // 2, me_k % 2
    occupied, orbitals = walkers.shape[1:]
    rows = block.shape[0] // 2
    vectors = rows // occupied
    share = rows // (2 * CHUNKS)
    part = orbitals // (2 * wide)
    steps = deep - 1
    far = 2 + steps
    cut = occupied // CHUNKS

    def on_line(distance, flip):
        position = ((hi + distance) % deep) * 2 + (lo + flip) % 2
        return (position * 2 + y, me_k)

    def on_plane(flip, distance):
        return ((hi * 2 + lo) * 2 + (y + flip) % 2, ((x + distance) % wide) * 2 + core)

    near = on_line(0, 1)
    pair = on_plane(1, 0)
    mate = (me_c, x * 2 + (1 - core))
    units = [(flip, j) for flip in (1, 0) for j in reversed(range(wide))]

    load_green = pltpu.make_async_copy(green_hbm.at[0], walkers.at[0], load_sem.at[0])
    load_chol = [
        pltpu.make_async_copy(
            chol_hbm.at[v], block.at[pl.ds(v * occupied, occupied)], load_sem.at[1 + v]
        )
        for v in range(vectors)
    ]
    load_green.start()
    for load in load_chol:
        load.start()

    barrier = pltpu.get_barrier_semaphore()

    def greet(device):
        pl.semaphore_signal(barrier, inc=1, device_id=device, device_id_type=MESH)

    greet(near)
    greet(mate)

    def greet_line(s):
        greet(on_line(s + 1, 0))
        greet(on_line(s + 1, 1))

    each(steps, greet_line)
    for flip, j in units[:-1]:
        greet(on_plane(flip, j))
    weight = weight_ref[0]
    weight_tile[...] = jnp.full(weight_tile.shape, weight, F32)
    pl.semaphore_wait(barrier, 2 + 2 * steps + len(units) - 1)

    def remote(src, dst, sems, index, device):
        return pltpu.make_async_remote_copy(
            src_ref=src, dst_ref=dst, send_sem=sems.at[0, index], recv_sem=sems.at[1, index],
            device_id=device, device_id_type=MESH,
        )

    def send_half(p):
        start = (2 * p + core) * share
        src = pl.ds(pl.multiple_of(start, share), share)
        dst = pl.ds(pl.multiple_of(rows + start, share), share)
        return remote(block.at[src], block.at[dst], half_sem, p, pair)

    def send_share(p):
        at = pl.ds(pl.multiple_of(rows + (2 * p + core) * share, share), share)
        return remote(block.at[at], block.at[at], share_sem, p, mate)

    send_near = remote(walkers.at[0], walkers.at[1], near_sem, 0, near)
    send_near_weight = remote(weight_tile, weights.at[0], weight_sem, 0, near)
    send_near_cot = remote(near_out, near_in, near_cot_sem, 0, near)

    def send_hi(s, p):
        at = pl.ds(p * cut, cut)
        return remote(
            walkers.at[0, at], walkers.at[2 + s, at], hi_sem, s * CHUNKS + p, on_line(s + 1, 0)
        )

    def send_far(s, p):
        at = pl.ds(p * cut, cut)
        return remote(
            walkers.at[2 + s, at], walkers.at[far + s, at], far_sem, s * CHUNKS + p, near
        )

    def send_weight(s, flip):
        slot = 1 + s + flip * steps
        return remote(weight_tile, weights.at[slot], weight_sem, slot, on_line(s + 1, flip))

    def send_far_cot(s, p):
        at = pl.ds(p * cut, cut)
        owner = near if p < SUMMED else on_line(deep - 1 - s, 1)
        return remote(far_out.at[s, at], far_in.at[s, at], far_cot_sem, s * CHUNKS + p, owner)

    def send_hi_cot(s, p):
        at = pl.ds(p * cut, cut)
        return remote(
            hi_out.at[s, at], hi_in.at[s, at], hi_cot_sem, s * CHUNKS + p, on_line(deep - 1 - s, 0)
        )

    def send_mate(u):
        return remote(mate_out.at[u], mate_in.at[u], mate_sem, u, mate)

    def send_grad(u):
        return remote(grad_out.at[u], grad_in.at[u], grad_sem, u, on_plane(*units[u]))

    load_green.wait()
    for p in range(CHUNKS):
        each(steps, lambda s: send_hi(s, p).start())
    for load in load_chol:
        load.wait()
    for p in range(CHUNKS):
        send_half(p).start()

    def start_weights(s):
        send_weight(s, 0).start()
        send_weight(s, 1).start()

    each(steps, start_weights)

    def meet(first, count, base, size):
        held = block[pl.ds(base, size), :]
        stack = walkers[pl.ds(first, count)].reshape(count * occupied, orbitals)
        swapped = lax.dot_general(held, stack, NT, preferred_element_type=F32).astype(BF16)
        pieces = [
            [
                swapped[v * occupied:(v + 1) * occupied, w * occupied:(w + 1) * occupied]
                for v in range(size // occupied)
            ]
            for w in range(count)
        ]
        wide_rows = [jnp.concatenate(line, axis=1) for line in pieces]
        cots = jnp.dot(jnp.concatenate(wide_rows, axis=0), held, preferred_element_type=F32)
        return cots.reshape(count, occupied, orbitals), pieces

    def gradients(first, scales, base, size, pieces, fresh):
        term = None
        for w, scale in enumerate(scales):
            tall = jnp.concatenate([piece.T for piece in pieces[w]], axis=0)
            more = scale * jnp.dot(tall, walkers[first + w], preferred_element_type=F32)
            term = more if term is None else term + more
        at = pl.ds(base, size)
        if fresh:
            total[at, :] = term
        else:
            total[at, :] += term

    def scale_of(slot):
        return weights[slot][0:1, 0:1]

    cots, pieces = meet(0, 1, 0, rows)
    early_cot[0] = cots[0]
    gradients(0, [weight], 0, rows, pieces, True)

    for p in range(CHUNKS):
        def pass_green(s):
            send_hi(s, p).wait_recv()
            send_far(s, p).start()

        each(steps, pass_green)
        if p == 0:
            send_near.start()
            send_near_weight.start()
        send_half(p).wait_recv()
        send_share(p).start()

    send_near.wait_recv()
    send_near_weight.wait_recv()
    each(steps, lambda s: send_weight(s, 0).wait_recv())
    group = min(far, 3)
    scales = [weight] + [scale_of(w) for w in range(group - 1)]
    cots, pieces = meet(1, group - 1, 0, rows)
    early_cot[1:group] = cots
    gradients(1, scales[1:], 0, rows, pieces, False)

    def meet_hi(s):
        cots, pieces = meet(group + s, 1, 0, rows)
        early_cot[group + s] = cots[0]
        gradients(group + s, [scale_of(group + s - 1)], 0, rows, pieces, False)

    each(far - group, meet_hi)
    for p in range(CHUNKS):
        send_share(p).wait_recv()
        base = rows + 2 * p * share
        cots, pieces = meet(0, group, base, 2 * share)
        early_cot[0:group] += cots
        if p == CHUNKS - 1:
            near_out[...] = early_cot[1].astype(BF16)
            send_near_cot.start()

            def send_home(s):
                for p in range(SUMMED, CHUNKS):
                    at = pl.ds(p * cut, cut)
                    hi_out[s, at] = early_cot[2 + s, at].astype(BF16)
                    send_hi_cot(s, p).start()

            each(group - 2, send_home)
        gradients(0, scales, base, 2 * share, pieces, True)

        def finish_hi(s):
            cots, pieces = meet(group + s, 1, base, 2 * share)
            early_cot[group + s] += cots[0]
            if p == CHUNKS - 1:
                send_home(group - 2 + s)
            gradients(group + s, [scale_of(group + s - 1)], base, 2 * share, pieces, False)

        each(far - group, finish_hi)

    def piece_of(unit, of_core):
        flip, j = unit
        column = pl.multiple_of((((x + j) % wide) * 2 + of_core) * part, part)
        return total[pl.ds(flip * rows, rows), pl.ds(column, part)]

    def meet_far(s, last):
        for p in range(CHUNKS):
            send_far(s, p).wait_recv()
        send_weight(s, 1).wait_recv()
        cots, pieces = meet(far + s, 1, 0, 2 * rows)
        far_out[s] = cots[0].astype(BF16)
        for p in range(CHUNKS):
            send_far_cot(s, p).start()
        for flip in (1, 0):
            chosen = [pieces[0][flip * vectors:(flip + 1) * vectors]]
            gradients(far + s, [scale_of(far - 1 + s)], flip * rows, rows, chosen, False)
            if last:
                for u, unit in enumerate(units):
                    if unit[0] == flip:
                        mate_out[u] = piece_of(unit, 1 - core).astype(BF16)
                        send_mate(u).start()

    each(steps - 1, lambda s: meet_far(s, False))
    meet_far(steps - 1, True)

    def pass_cots(p):
        at = pl.ds(p * cut, cut)

        def pass_cot(s):
            send_far_cot(s, p).wait_recv()
            hi_out[s, at] = (early_cot[2 + s, at] + far_in[s, at].astype(F32)).astype(BF16)
            send_hi_cot(s, p).start()

        each(steps, pass_cot)

    for u, unit in enumerate(units[:-1]):
        send_mate(u).wait_recv()
        grad_out[u] = (piece_of(unit, core) + mate_in[u].astype(F32)).astype(BF16)
        send_grad(u).start()
        if u == 0:
            for p in range(SUMMED):
                pass_cots(p)

    last = len(units) - 1
    send_mate(last).wait_recv()
    grad = piece_of(units[last], core) + mate_in[last].astype(F32)
    send_near_cot.wait_recv()
    early_cot[0] += near_in[...].astype(F32)
    for u in range(last):
        send_grad(u).wait_recv()
        grad += grad_in[u].astype(F32)
    grad_ref[...] = grad.reshape(vectors, occupied, part)

    def add_hi(s):
        for p in range(CHUNKS):
            send_hi_cot(s, p).wait_recv()
        early_cot[0] += hi_in[s].astype(F32)
        for p in range(SUMMED, CHUNKS):
            at = pl.ds(p * cut, cut)
            send_far_cot(s, p).wait_recv()
            early_cot[0, at] += far_in[s, at].astype(F32)

    each(steps, add_hi)
    cot_ref[0] = weight * early_cot[0]

    for copy in (send_near, send_near_weight, send_near_cot):
        copy.wait_send()
    for p in range(CHUNKS):
        send_half(p).wait_send()
        send_share(p).wait_send()

    def finish(s):
        send_weight(s, 0).wait_send()
        send_weight(s, 1).wait_send()
        for p in range(CHUNKS):
            for send in (send_hi, send_far, send_far_cot, send_hi_cot):
                send(s, p).wait_send()

    each(steps, finish)
    for u in range(len(units)):
        send_mate(u).wait_send()
    for u in range(last):
        send_grad(u).wait_send()


def hand_over(cot, grad, cot_out, grad_out):
    cot_out[...] = -cot[...]
    grad_out[...] = -grad[...]


def shards(green, chol, weight):
    deep = lax.axis_size("chol") // 4
    wide = lax.axis_size("walk") // 2
    vectors, occupied, orbitals = chol.shape
    rows = vectors * occupied
    part = orbitals // (2 * wide)
    steps = deep - 1
    units = 2 * wide
    matrix = (occupied, orbitals)
    vmem = pl.BlockSpec(memory_space=pltpu.VMEM)
    anywhere = pl.BlockSpec(memory_space=pl.ANY)
    dma = pltpu.SemaphoreType.DMA
    out_shape = (
        jax.ShapeDtypeStruct((1, occupied, orbitals), F32),
        jax.ShapeDtypeStruct((vectors, occupied, part), F32),
    )
    cot, grad = pl.pallas_call(
        functools.partial(kernel, deep, wide),
        out_shape=out_shape,
        in_specs=[pl.BlockSpec(memory_space=pltpu.SMEM), anywhere, anywhere],
        out_specs=(vmem, vmem),
        scratch_shapes=[
            pltpu.VMEM((2 * deep,) + matrix, BF16),
            pltpu.VMEM((2 * rows, orbitals), BF16),
            pltpu.VMEM((8, 128), F32),
            pltpu.VMEM((1 + 2 * steps, 8, 128), F32),
            pltpu.VMEM((2 * rows, orbitals), F32),
            pltpu.VMEM((2 + steps,) + matrix, F32),
            pltpu.VMEM(matrix, BF16),
            pltpu.VMEM(matrix, BF16),
            pltpu.VMEM((steps,) + matrix, BF16),
            pltpu.VMEM((steps,) + matrix, BF16),
            pltpu.VMEM((steps,) + matrix, BF16),
            pltpu.VMEM((steps,) + matrix, BF16),
            pltpu.VMEM((units, rows, part), BF16),
            pltpu.VMEM((units, rows, part), BF16),
            pltpu.VMEM((units - 1, rows, part), BF16),
            pltpu.VMEM((units - 1, rows, part), BF16),
            dma((1 + vectors,)), dma((2, CHUNKS)), dma((2, CHUNKS)), dma((2, 1)),
            dma((2, steps * CHUNKS)), dma((2, steps * CHUNKS)),
            dma((2, 1 + 2 * steps)), dma((2, 1)),
            dma((2, steps * CHUNKS)), dma((2, steps * CHUNKS)),
            dma((2, units)), dma((2, units - 1)),
        ],
        compiler_params=pltpu.CompilerParams(
            collective_id=0, has_side_effects=True, vmem_limit_bytes=VMEM_BYTES
        ),
    )(weight, green, chol)
    return pl.pallas_call(
        hand_over,
        out_shape=out_shape,
        in_specs=[vmem, vmem],
        out_specs=(vmem, vmem),
        compiler_params=pltpu.CompilerParams(vmem_limit_bytes=VMEM_BYTES),
    )(cot, grad)


def solution(mesh):
    in_specs = (P(("chol", "walk"), None, None), P("chol", None, None), P(("chol", "walk")))
    out_specs = (P(("chol", "walk"), None, None), P("chol", None, "walk"))
    return jax.shard_map(shards, mesh=mesh, in_specs=in_specs, out_specs=out_specs, check_vma=False)
```
